256 devices in a mesh: pair: 64 (over y, z, x_hi), row: 4 (over x_lo, core).
Axes of the slice: x: 4 (x_hi: 2, x_lo: 2; x = x_hi * 2 + x_lo), y: 4, z: 8, core: 2. Of those that a mesh axis runs over, the one named last changes fastest.
Arguments:
- matrix: float32 [8192, 16384], P('row', 'pair'), may hold values from -8.75 to 8.75
- vectors: float32 [4096, 16384], P('row', 'pair'), may hold values from -6 to 6
Outputs:
- matrix_out: float32 [8192, 16384], P('row', 'pair')
- vectors_out: float32 [4096, 16384], P('row', 'pair')
- off_mass: float32 [2], replicated
The draws below stay inside these ranges and needn't reach their ends.
All inputs are finite; a program needn't handle non-finite values.
Results may differ from the reference program's by a relative error of at most 0.00021.
Values sent between devices are 32-bit elements; how exact they have to be, the bound alone decides.
A program may use at most 64 MiB of HBM per device.

```python
import math
import jax
import jax.numpy as jnp
from jax import lax

BLK = 128
ORTH = 2
M = 8192
VROWS = 4096
N = 16384


def draw_matrix(key, part):
    key = jax.random.fold_in(key, 11)
    key_entries, key_scales = jax.random.split(key)
    column = jnp.arange(N, dtype=jnp.float32) / N
    entries = jnp.clip(jax.random.normal(key_entries, (M, N), jnp.float32), -5.0, 5.0)
    ramp = 1.0 + 0.4 * column
    spread = jnp.exp(jax.random.uniform(key_scales, (N,), jnp.float32, math.log(0.8), math.log(1.25)))
    return entries * (ramp * spread)[None, :]


def block_scale(rng, shape, shards, least, largest):
    level, own = 1.0, jax.random.fold_in(rng, 6)
    for axis_at, parts in shards:
        steps = jnp.exp(jax.random.uniform(jax.random.fold_in(own, axis_at), (parts,), jnp.float32, least / len(shards), largest / len(shards)))
        level = level * jnp.repeat(steps, shape[axis_at] // parts).reshape([-1 if axis == axis_at else 1 for axis in range(len(shape))])
    return level


def noise(stream_key, dims, scale, limit, pieces=(), kind=jnp.bfloat16):
    level = block_scale(stream_key, dims, pieces, -0.22, 0.18) if pieces else 1.0
    result = jax.random.normal(stream_key, dims, jnp.float32) * scale * level
    return jnp.minimum(jnp.maximum(result, -limit), limit).astype(kind)


def setup_inputs(seed: int = 0) -> dict:
    arg_keys = jax.random.split(jax.random.key(seed), 3)
    return {
        "matrix": draw_matrix(jax.random.fold_in(arg_keys[2], 71), 0),
        "vectors": noise(arg_keys[1], (VROWS, N), 1.0, 6.0, ((0, 4), (1, 64)), jnp.float32),
    }


HIGH = lax.Precision.HIGHEST

def rotation(gram_matrix):
    current = gram_matrix
    rotated = gram_matrix
    for iteration in range(ORTH):
        product = jnp.dot(current.T, current, precision=HIGH)
        factor = jnp.linalg.cholesky(product)
        rotated = lax.linalg.triangular_solve(factor, current, left_side=False, lower=True, transpose_a=True)
        if iteration + 1 < ORTH:
            current = jnp.dot(gram_matrix, rotated, precision=HIGH)
    return rotated

def off_term(gram_matrix):
    outside = 1.0 - jnp.eye(gram_matrix.shape[0], dtype=jnp.float32)
    return jnp.sum(gram_matrix * gram_matrix * outside)

def one_slot(blocks):
    slot_a, slot_v = blocks
    gram_matrix = jnp.dot(slot_a.T, slot_a, precision=HIGH)
    turned = rotation(gram_matrix)
    return (jnp.dot(slot_a, turned, precision=HIGH), jnp.dot(slot_v, turned, precision=HIGH), off_term(gram_matrix))

def move_blocks(slots):
    tops = slots[:, :, :BLK]
    bottoms = slots[:, :, BLK:]
    new_top = jnp.concatenate([tops[0:1], bottoms[0:1], tops[1:-1]], axis=0)
    new_bottom = jnp.concatenate([bottoms[1:], tops[-1:]], axis=0)
    return jnp.concatenate([new_top, new_bottom], axis=2)

def reference(matrix, vectors):
    pairs = N // (2 * BLK)
    rows_a = matrix.shape[0]
    rows_v = vectors.shape[0]
    slots_a = matrix.reshape(rows_a, pairs, 2 * BLK).transpose(1, 0, 2)
    slots_v = vectors.reshape(rows_v, pairs, 2 * BLK).transpose(1, 0, 2)
    slots_a, slots_v, mass_one = lax.map(one_slot, (slots_a, slots_v))
    slots_a = move_blocks(slots_a)
    slots_v = move_blocks(slots_v)
    slots_a, slots_v, mass_two = lax.map(one_slot, (slots_a, slots_v))
    scale = 1.0 / (float(rows_a) * float(rows_a) * float(pairs))
    off_mass = jnp.stack([jnp.sum(mass_one), jnp.sum(mass_two)]) * scale
    matrix_out = slots_a.transpose(1, 0, 2).reshape(rows_a, N)
    vectors_out = slots_v.transpose(1, 0, 2).reshape(rows_v, N)
    return (matrix_out, vectors_out, off_mass)
```

```python
import functools

import jax
import jax.numpy as jnp
from jax import lax
from jax.experimental import pallas as pl
from jax.experimental.pallas import tpu as pltpu
from jax.sharding import PartitionSpec as P

HIGH = lax.Precision.HIGHEST
MESH = pl.DeviceIdType.MESH
F32 = jnp.float32
BLK = 128
WIDE = 2 * BLK
OUTER = 32
CHUNK = 256
CORRECT = 1


def dot(a, b, ca, cb):
    dims = (((ca,), (cb,)), ((), ()))
    return lax.dot_general(a, b, dims, precision=HIGH, preferred_element_type=F32)


def bdot(a, b, ca, cb):
    dims = (((ca,), (cb,)), ((), ()))
    return lax.dot_general(a, b, dims, preferred_element_type=F32)


def halves(a):
    high = a.astype(jnp.bfloat16)
    return high, (a - high.astype(F32)).astype(jnp.bfloat16)


def dot3(a, b, ca, cb):
    ah, al = halves(a)
    bh, bl = halves(b)
    return bdot(al, bh, ca, cb) + bdot(ah, bl, ca, cb) + bdot(ah, bh, ca, cb)


def wide(v):
    return jnp.concatenate([v] * (WIDE // 128), axis=1)


def panel(s, splat, k, end):
    c0 = (k // 128) * 128
    own = s[pl.ds(k, 8), pl.ds(c0, 128)]
    for j in range(8):
        at = k - c0 + j
        splat[j] = jnp.broadcast_to(own[:, at : at + 1], (8, 128))
    e = {(i, j): splat[j, i : i + 1, :] for j in range(8) for i in range(j, 8)}
    lanes = lax.broadcasted_iota(jnp.int32, (1, WIDE), 1)
    rows = []
    for i in range(8):
        row = s[pl.ds(k + i, 1), :]
        row = jnp.where((lanes >= k) & (lanes < k + 8), 0.0, row)
        rows.append(jnp.where(lanes == k + i, 1.0, row))
    l = {}
    scale = []
    for a in range(0, 8, 2):
        b = a + 1
        p, q, t = e[a, a], e[b, a], e[b, b]
        ra, rd = lax.rsqrt(p), lax.rsqrt(p * t - q * q)
        rb = rd * (p * ra)
        scale += [ra, rb]
        l[b, a] = q * ra
        for i in range(b + 1, 8):
            l[i, a] = e[i, a] * ra
            l[i, b] = (e[i, b] - l[i, a] * l[b, a]) * rb
        for j in range(b + 1, 8):
            for i in range(j, 8):
                e[i, j] = e[i, j] - (l[i, a] * l[j, a] + l[i, b] * l[j, b])
        rows[a] = rows[a] * wide(ra)
        rows[b] = (rows[b] - wide(l[b, a]) * rows[a]) * wide(rb)
        for i in range(b + 1, 8):
            rows[i] = rows[i] - (wide(l[i, a]) * rows[a] + wide(l[i, b]) * rows[b])
    for i in range(8):
        s[pl.ds(k + i, 1), :] = rows[i]
    full = [jnp.broadcast_to(row, (8, WIDE)) for row in rows]
    lanes = lax.broadcasted_iota(jnp.int32, (8, WIDE), 1)
    inside = (lanes >= k) & (lanes < k + 8)
    for g in range(k + 8, end, 8):
        old = s[pl.ds(g, 8), :]
        m = []
        for j in range(8):
            at = k + j
            t = jnp.broadcast_to(old[:, at : at + 1], (8, 128))
            for jj in range(j):
                t = t - m[jj] * jnp.broadcast_to(l[j, jj], (8, 128))
            m.append(t * jnp.broadcast_to(scale[j], (8, 128)))
        new = jnp.where(inside, 0.0, old)
        for j in range(8):
            new = new - wide(m[j]) * full[j]
        s[pl.ds(g, 8), :] = new


def factor_inverse(s, splat):
    for b0 in range(0, WIDE, OUTER):
        b1 = b0 + OUTER
        for k in range(b0, b1, 8):
            panel(s, splat, k, b1)
        if b1 == WIDE:
            break
        lanes = lax.broadcasted_iota(jnp.int32, (OUTER, WIDE), 1)
        row = lax.broadcasted_iota(jnp.int32, (OUTER, WIDE), 0)
        block = jnp.where((lanes < b1) & (lanes > row + b0), 0.0, s[pl.ds(b0, OUTER), :])
        rest = s[pl.ds(b1, WIDE - b1), :]
        c0 = (b0 // 128) * 128
        near = lax.broadcasted_iota(jnp.int32, (1, 128), 1) + c0
        inverse = jnp.where((near >= b0) & (near < b1), block[:, c0 : c0 + 128], 0.0)
        factor = dot3(rest[:, c0 : c0 + 128], inverse, 1, 1)
        lanes = lax.broadcasted_iota(jnp.int32, (1, WIDE), 1)
        rest = jnp.where((lanes >= b0) & (lanes < b1), 0.0, rest)
        s[pl.ds(b1, WIDE - b1), :] = rest - dot3(factor, block, 1, 0)


def rotation(gram, s, splat):
    square = dot(gram, gram, 1, 0)
    s[...] = dot(square, square, 1, 0)
    factor_inverse(s, splat)
    row = lax.broadcasted_iota(jnp.int32, (WIDE, WIDE), 0)
    col = lax.broadcasted_iota(jnp.int32, (WIDE, WIDE), 1)
    turn = dot(square, jnp.where(row >= col, s[...], 0.0), 1, 1)
    for _ in range(CORRECT):
        over = dot(turn, turn, 0, 0)
        over = jnp.where(row == col, (over - 1.0) * 0.5, jnp.where(row < col, over, 0.0))
        turn = turn - dot(turn, over, 1, 0)
    return turn


def kernel(
    pairs, gram_scale, mass_scale,
    a_ref, v_ref, ao_ref, vo_ref, m_ref,
    sent, got, done, s, splat, hh, hl, qh, ql,
    part, near, half, far, full, mine, groups,
    up_s, up_r, dn_s, dn_r, sum_s, sum_r, grp_s, grp_r, out_sem,
):
    rows_a, rows_v = a_ref.shape[0], v_ref.shape[0]
    chunks_a, chunks = rows_a // CHUNK, (rows_a + rows_v) // CHUNK
    inner = min(8, pairs)
    outer = pairs // inner
    p, r = lax.axis_index("pair"), lax.axis_index("row")
    core = lax.rem(r, 2)
    beside = r + 1 - 2 * core
    across = lax.rem(r + 2, 4)
    pa, pb = p // inner, lax.rem(p, inner)
    up_from = (pairs - p) // pairs
    has_up, has_dn = p < pairs - 1, p > 0

    def group_device(stage, other):
        return (pa * inner + other, r) if stage == 0 else (other * inner + pb, r)

    sizes, place = (inner, outer), (pb, pa)

    bar = pltpu.get_barrier_semaphore()

    def hello(device):
        pl.semaphore_signal(bar, 1, device_id=device, device_id_type=MESH)

    hello((p, beside))
    hello((p, across))
    for stage in range(2):
        for k in range(1, sizes[stage]):
            hello(group_device(stage, lax.rem(place[stage] + k, sizes[stage])))

    @pl.when(has_up)
    def _():
        hello((p + 1, r))

    @pl.when(has_dn)
    def _():
        hello((p - 1, r))

    def add_gram(x):
        high, low = halves(x)
        hh[...] += bdot(high, high, 0, 0)
        hl[...] += bdot(high, low, 0, 0)

    def clear_gram():
        hh[...] = jnp.zeros_like(hh)
        hl[...] = jnp.zeros_like(hl)

    def sum_over_row(rnd):
        cross = hl[...]
        gram = hh[...] + (cross + cross.T)
        part[rnd, 0, pl.ds(0, 128), :] = gram[:128, :128]
        part[rnd, 0, pl.ds(128, 64), :] = gram[:64, 128:]
        part[rnd, 1, pl.ds(0, 64), :] = gram[64:128, 128:]
        part[rnd, 1, pl.ds(64, 128), :] = gram[128:, 128:]

        def move(step, src, dst, device):
            copy = pltpu.make_async_remote_copy(
                src_ref=src, dst_ref=dst, send_sem=sum_s.at[rnd, step], recv_sem=sum_r.at[rnd, step],
                device_id=device, device_id_type=MESH,
            )
            copy.start()
            copy.wait()

        if rnd == 0:
            ends = up_from + (p + 1) // pairs
            pl.semaphore_wait(bar, 2 + inner - 1 + outer - 1 + 2 - ends)

        move(0, part.at[rnd, 1 - core], near.at[rnd], (p, beside))
        half[rnd] = part[rnd, core] + near[rnd]
        move(1, half.at[rnd], far.at[rnd], (p, across))
        full[rnd, core] = half[rnd] + far[rnd]
        move(2, full.at[rnd, core], full.at[rnd, core], (p, beside))
        top = full[rnd, 0, pl.ds(0, 128), :]
        mid = jnp.concatenate([full[rnd, 0, pl.ds(128, 64), :], full[rnd, 1, pl.ds(0, 64), :]], axis=0)
        low = full[rnd, 1, pl.ds(64, 128), :]
        return jnp.concatenate(
            [jnp.concatenate([top, mid], axis=1), jnp.concatenate([mid.T, low], axis=1)], axis=0
        )

    def off_mass(gram):
        row = lax.broadcasted_iota(jnp.int32, (WIDE, WIDE), 0)
        col = lax.broadcasted_iota(jnp.int32, (WIDE, WIDE), 1)
        squares = jnp.where(row == col, 0.0, gram * gram)
        return jnp.sum(jnp.sum(squares, axis=1, keepdims=True), axis=0, keepdims=True)

    def take_turn(gram):
        high, low = halves(rotation(gram * gram_scale, s, splat))
        qh[...] = high
        ql[...] = low

    def turned(x):
        high, low = halves(x)
        return bdot(low, qh[...], 1, 0) + bdot(high, ql[...], 1, 0) + bdot(high, qh[...], 1, 0)

    def at(c):
        return pl.ds(pl.multiple_of(c * CHUNK, CHUNK), CHUNK)

    def up(c):
        return pltpu.make_async_remote_copy(
            src_ref=sent.at[up_from, at(c)], dst_ref=got.at[0, at(c)], send_sem=up_s.at[c], recv_sem=up_r.at[c],
            device_id=(p + 1, r), device_id_type=MESH,
        )

    def down(c):
        return pltpu.make_async_remote_copy(
            src_ref=sent.at[1, at(c)], dst_ref=got.at[1, at(c)], send_sem=dn_s.at[c], recv_sem=dn_r.at[c],
            device_id=(p - 1, r), device_id_type=MESH,
        )

    def send(c):
        @pl.when(has_up)
        def _():
            up(c).start()

        @pl.when(has_dn)
        def _():
            down(c).start()

    def receive(c):
        @pl.when(has_dn)
        def _():
            up(c).wait_recv()

        @pl.when(has_up)
        def _():
            down(c).wait_recv()

    def turn_chunk(c, x):
        y = turned(x)
        sent[0, at(c), :] = y[:, :BLK]
        sent[1, at(c), :] = y[:, BLK:]

        @pl.when(p == 0)
        def _():
            got[0, at(c), :] = y[:, :BLK]

        @pl.when(p == pairs - 1)
        def _():
            got[1, at(c), :] = y[:, :BLK]

    def arrived(c):
        return jnp.concatenate([got[0, at(c), :], got[1, at(c), :]], axis=1)

    def group_copy(stage, k):
        here = place[stage]
        other = lax.rem(here + k, sizes[stage])
        return pltpu.make_async_remote_copy(
            src_ref=mine.at[stage], dst_ref=groups.at[stage, here], send_sem=grp_s.at[stage, k],
            recv_sem=grp_r.at[stage, here], device_id=group_device(stage, other), device_id_type=MESH,
        )

    def group_send(stage, value):
        mine[stage] = value
        groups[stage, place[stage]] = value
        for k in range(1, sizes[stage]):
            group_copy(stage, k).start()

    def group_sum(stage):
        for k in range(1, sizes[stage]):
            other = lax.rem(place[stage] + k, sizes[stage])
            pltpu.make_async_remote_copy(
                src_ref=mine.at[stage], dst_ref=groups.at[stage, other], send_sem=grp_s.at[stage, k],
                recv_sem=grp_r.at[stage, other], device_id=group_device(stage, other), device_id_type=MESH,
            ).wait_recv()
        total = groups[stage, 0]
        for other in range(1, sizes[stage]):
            total = total + groups[stage, other]
        return total

    clear_gram()

    @pl.loop(0, chunks_a)
    def _(c):
        add_gram(a_ref[at(c), :])

    gram = sum_over_row(0)
    mass_one = off_mass(gram)
    take_turn(gram)

    @pl.loop(0, chunks_a)
    def _(c):
        turn_chunk(c, a_ref[at(c), :])
        send(c)

    @pl.loop(chunks_a, chunks)
    def _(c):
        turn_chunk(c, v_ref[at(c - chunks_a), :])

    clear_gram()
    late = chunks_a - (chunks - chunks_a)

    @pl.loop(0, late)
    def _(c):
        receive(c)
        add_gram(arrived(c))

    @pl.loop(late, chunks_a)
    def _(c):
        receive(c)
        send(c + chunks - chunks_a)
        add_gram(arrived(c))

    gram = sum_over_row(1)
    mass_two = off_mass(gram)
    first = lax.broadcasted_iota(jnp.int32, (8, 128), 1) == 0
    both = jnp.where(first, jnp.broadcast_to(mass_one, (8, 128)), jnp.broadcast_to(mass_two, (8, 128)))
    group_send(0, both)
    take_turn(gram)
    group_send(1, group_sum(0))

    def out(c):
        ref, c0 = (ao_ref, c) if c < chunks_a else (vo_ref, c - chunks_a)
        return pltpu.make_async_copy(done.at[at(c)], ref.at[pl.ds(c0 * CHUNK, CHUNK)], out_sem.at[c])

    for c in range(chunks):
        if c >= chunks_a:
            receive(c)
        done[at(c), :] = turned(arrived(c))
        out(c).start()
    m_ref[...] = group_sum(1) * mass_scale

    @pl.loop(0, chunks)
    def _(c):
        @pl.when(has_up)
        def _():
            up(c).wait_send()

        @pl.when(has_dn)
        def _():
            down(c).wait_send()

    for stage in range(2):
        for k in range(1, sizes[stage]):
            group_copy(stage, k).wait_send()
    for c in range(chunks):
        out(c).wait()


def local(pairs, matrix, vectors):
    rows_a, rows_v = matrix.shape[0], vectors.shape[0]
    total_rows = float(rows_a * lax.axis_size("row"))
    chunks = (rows_a + rows_v) // CHUNK
    inner = min(8, pairs)
    body = functools.partial(kernel, pairs, 2.0**-13, 1.0 / (total_rows * total_rows * float(pairs)))
    dma = pltpu.SemaphoreType.DMA
    vmem = pltpu.VMEM
    matrix_out, vectors_out, mass = pl.pallas_call(
        body,
        out_shape=(
            jax.ShapeDtypeStruct(matrix.shape, F32),
            jax.ShapeDtypeStruct(vectors.shape, F32),
            jax.ShapeDtypeStruct((8, 128), F32),
        ),
        in_specs=[pl.BlockSpec(memory_space=vmem)] * 2,
        out_specs=(
            pl.BlockSpec(memory_space=pl.ANY),
            pl.BlockSpec(memory_space=pl.ANY),
            pl.BlockSpec(memory_space=vmem),
        ),
        scratch_shapes=[
            vmem((2, rows_a + rows_v, BLK), F32),
            vmem((2, rows_a + rows_v, BLK), F32),
            vmem((rows_a + rows_v, WIDE), F32),
            vmem((WIDE, WIDE), F32),
            vmem((8, 8, 128), F32),
            vmem((WIDE, WIDE), F32),
            vmem((WIDE, WIDE), F32),
            vmem((WIDE, WIDE), jnp.bfloat16),
            vmem((WIDE, WIDE), jnp.bfloat16),
            vmem((2, 2, 192, 128), F32),
            vmem((2, 192, 128), F32),
            vmem((2, 192, 128), F32),
            vmem((2, 192, 128), F32),
            vmem((2, 2, 192, 128), F32),
            vmem((2, 8, 128), F32),
            vmem((2, 8, 8, 128), F32),
            dma((chunks,)),
            dma((chunks,)),
            dma((chunks,)),
            dma((chunks,)),
            dma((2, 3)),
            dma((2, 3)),
            dma((2, 8)),
            dma((2, 8)),
            dma((chunks,)),
        ],
        compiler_params=pltpu.CompilerParams(
            collective_id=0, has_side_effects=True, vmem_limit_bytes=40 * 2**20
        ),
    )(matrix, vectors)
    return matrix_out, vectors_out, mass[0, :2]


def solution(mesh):
    return jax.shard_map(
        functools.partial(local, mesh.shape["pair"]),
        mesh=mesh,
        in_specs=(P("row", "pair"), P("row", "pair")),
        out_specs=(P("row", "pair"), P("row", "pair"), P()),
        check_vma=False,
    )
```

```python
import functools

import jax
import jax.numpy as jnp
from jax import lax
from jax.experimental import pallas as pl
from jax.experimental.pallas import tpu as pltpu
from jax.sharding import PartitionSpec as P

HIGH = lax.Precision.HIGHEST
MESH = pl.DeviceIdType.MESH
F32 = jnp.float32
BLK = 128
WIDE = 2 * BLK
OUTER = 32
PIECE = 512
CHUNK = 256
SMALL = 128
RAW = 3
RAW_FIRST = 128
EARLY = 1
MIDDLE = 1
CORRECT = 1


def dot(a, b, ca, cb):
    dims = (((ca,), (cb,)), ((), ()))
    return lax.dot_general(a, b, dims, precision=HIGH, preferred_element_type=F32)


def bdot(a, b, ca, cb):
    dims = (((ca,), (cb,)), ((), ()))
    return lax.dot_general(a, b, dims, preferred_element_type=F32)


def halves(a):
    high = a.astype(jnp.bfloat16)
    return high, (a - high.astype(F32)).astype(jnp.bfloat16)


def dot3(a, b, ca, cb):
    ah, al = halves(a)
    bh, bl = halves(b)
    return bdot(al, bh, ca, cb) + bdot(ah, bl, ca, cb) + bdot(ah, bh, ca, cb)


def wide(v):
    return jnp.concatenate([v] * (WIDE // 128), axis=1)


def panel(s, splat, k, end):
    c0 = (k // 128) * 128
    own = s[pl.ds(k, 8), pl.ds(c0, 128)]
    for j in range(8):
        at = k - c0 + j
        splat[j] = jnp.broadcast_to(own[:, at : at + 1], (8, 128))
    e = {(i, j): splat[j, i : i + 1, :] for j in range(8) for i in range(j, 8)}
    lanes = lax.broadcasted_iota(jnp.int32, (1, WIDE), 1)
    rows = []
    for i in range(8):
        row = s[pl.ds(k + i, 1), :]
        row = jnp.where((lanes >= k) & (lanes < k + 8), 0.0, row)
        rows.append(jnp.where(lanes == k + i, 1.0, row))
    l = {}
    scale = []
    for a in range(0, 8, 2):
        b = a + 1
        p, q, t = e[a, a], e[b, a], e[b, b]
        ra, rd = lax.rsqrt(p), lax.rsqrt(p * t - q * q)
        rb = rd * (p * ra)
        scale += [ra, rb]
        l[b, a] = q * ra
        for i in range(b + 1, 8):
            l[i, a] = e[i, a] * ra
            l[i, b] = (e[i, b] - l[i, a] * l[b, a]) * rb
        for j in range(b + 1, 8):
            for i in range(j, 8):
                e[i, j] = e[i, j] - (l[i, a] * l[j, a] + l[i, b] * l[j, b])
        rows[a] = rows[a] * wide(ra)
        rows[b] = (rows[b] - wide(l[b, a]) * rows[a]) * wide(rb)
        for i in range(b + 1, 8):
            rows[i] = rows[i] - (wide(l[i, a]) * rows[a] + wide(l[i, b]) * rows[b])
    for i in range(8):
        s[pl.ds(k + i, 1), :] = rows[i]
    full = [jnp.broadcast_to(row, (8, WIDE)) for row in rows]
    lanes = lax.broadcasted_iota(jnp.int32, (8, WIDE), 1)
    inside = (lanes >= k) & (lanes < k + 8)
    for g in range(k + 8, end, 8):
        old = s[pl.ds(g, 8), :]
        m = []
        for j in range(8):
            at = k + j
            t = jnp.broadcast_to(old[:, at : at + 1], (8, 128))
            for jj in range(j):
                t = t - m[jj] * jnp.broadcast_to(l[j, jj], (8, 128))
            m.append(t * jnp.broadcast_to(scale[j], (8, 128)))
        new = jnp.where(inside, 0.0, old)
        for j in range(8):
            new = new - wide(m[j]) * full[j]
        s[pl.ds(g, 8), :] = new


def factor_inverse(s, splat):
    for b0 in range(0, WIDE, OUTER):
        b1 = b0 + OUTER
        for k in range(b0, b1, 8):
            panel(s, splat, k, b1)
        if b1 == WIDE:
            break
        lanes = lax.broadcasted_iota(jnp.int32, (OUTER, WIDE), 1)
        row = lax.broadcasted_iota(jnp.int32, (OUTER, WIDE), 0)
        block = jnp.where((lanes < b1) & (lanes > row + b0), 0.0, s[pl.ds(b0, OUTER), :])
        rest = s[pl.ds(b1, WIDE - b1), :]
        c0 = (b0 // 128) * 128
        near = lax.broadcasted_iota(jnp.int32, (1, 128), 1) + c0
        inverse = jnp.where((near >= b0) & (near < b1), block[:, c0 : c0 + 128], 0.0)
        factor = dot3(rest[:, c0 : c0 + 128], inverse, 1, 1)
        lanes = lax.broadcasted_iota(jnp.int32, (1, WIDE), 1)
        rest = jnp.where((lanes >= b0) & (lanes < b1), 0.0, rest)
        s[pl.ds(b1, WIDE - b1), :] = rest - dot3(factor, block, 1, 0)


def rotation(gram, s, splat):
    square = dot(gram, gram, 1, 0)
    s[...] = dot(square, square, 1, 0)
    factor_inverse(s, splat)
    row = lax.broadcasted_iota(jnp.int32, (WIDE, WIDE), 0)
    col = lax.broadcasted_iota(jnp.int32, (WIDE, WIDE), 1)
    turn = dot(square, jnp.where(row >= col, s[...], 0.0), 1, 1)
    for _ in range(CORRECT):
        over = dot(turn, turn, 0, 0)
        over = jnp.where(row == col, (over - 1.0) * 0.5, jnp.where(row < col, over, 0.0))
        turn = turn - dot(turn, over, 1, 0)
    return turn


def kernel(
    pairs, gram_scale, mass_scale,
    a_ref, v_ref, ao_ref, vo_ref, m_ref,
    held, sent, got, done, raw, relayed, s, splat, hh, hl, qh, ql, ph, pl_, q_out, q_in,
    part, near, half, far, full, mine, groups,
    in_sem, up_s, up_r, dn_s, dn_r, raw_s, raw_r, rel_s, rel_r, turn_s, turn_r, sum_s, sum_r, grp_s, grp_r, out_sem,
):
    rows_a, rows_v = a_ref.shape[0], v_ref.shape[0]
    chunks_a, small = rows_a // CHUNK, rows_v // SMALL
    inner = min(8, pairs)
    outer = pairs // inner
    p, r = lax.axis_index("pair"), lax.axis_index("row")
    core = lax.rem(r, 2)
    beside = r + 1 - 2 * core
    across = lax.rem(r + 2, 4)
    odd = lax.rem(p, 2)
    mate = p + 1 - 2 * odd
    to = p + 2 - 4 * odd
    source = p - 2 + 4 * odd
    pa, pb = p // inner, lax.rem(p, inner)
    up_from = (pairs - p) // pairs
    has_up, has_dn = p < pairs - 1, p > 0
    has_to = (to >= 0) & (to < pairs)
    has_source = (source >= 0) & (source < pairs)

    def group_device(stage, other):
        return (pa * inner + other, r) if stage == 0 else (other * inner + pb, r)

    sizes, place = (inner, outer), (pb, pa)

    def remote(src, dst, send_sem, recv_sem, device):
        return pltpu.make_async_remote_copy(
            src_ref=src, dst_ref=dst, send_sem=send_sem, recv_sem=recv_sem, device_id=device, device_id_type=MESH
        )

    bar = pltpu.get_barrier_semaphore()

    def hello(device):
        pl.semaphore_signal(bar, 1, device_id=device, device_id_type=MESH)

    hello((p, beside))
    hello((p, across))
    for stage in range(2):
        for k in range(1, sizes[stage]):
            hello(group_device(stage, lax.rem(place[stage] + k, sizes[stage])))

    for there, device in ((has_up, p + 1), (has_dn, p - 1), (has_to, to), (has_source, source)):

        @pl.when(there)
        def _(device=device):
            hello((device, r))

    def barrier():
        ends = up_from + (p + 1) // pairs
        ends = ends + (pairs + 1 - p) // pairs + (p + 2) // pairs
        pl.semaphore_wait(bar, 2 + inner - 1 + outer - 1 + 4 - ends)

    def rows(c, size=CHUNK):
        return pl.ds(pl.multiple_of(c * size, size), size)

    pieces = rows_a // PIECE

    def load(i):
        src = a_ref.at[rows(i, PIECE)] if i < pieces else v_ref
        size = PIECE if i < pieces else rows_v
        return pltpu.make_async_copy(src, held.at[pl.ds(i * PIECE, size)], in_sem.at[i])

    for i in range(pieces + 1):
        load(i).start()

    def add_gram(x):
        high, low = halves(x)
        hh[...] += bdot(high, high, 0, 0)
        hl[...] += bdot(high, low, 0, 0)

    def clear_gram():
        hh[...] = jnp.zeros_like(hh)
        hl[...] = jnp.zeros_like(hl)

    def sum_over_row(rnd, between):
        cross = hl[...]
        gram = hh[...] + (cross + cross.T)
        part[rnd, 0, pl.ds(0, 128), :] = gram[:128, :128]
        part[rnd, 0, pl.ds(128, 64), :] = gram[:64, 128:]
        part[rnd, 1, pl.ds(0, 64), :] = gram[64:128, 128:]
        part[rnd, 1, pl.ds(64, 128), :] = gram[128:, 128:]

        def move(step, src, dst, device):
            return remote(src, dst, sum_s.at[rnd, step], sum_r.at[rnd, step], device)

        copy = move(0, part.at[rnd, 1 - core], near.at[rnd], (p, beside))
        copy.start()
        copy.wait()
        half[rnd] = part[rnd, core] + near[rnd]
        copy = move(1, half.at[rnd], far.at[rnd], (p, across))
        copy.start()
        between()
        copy.wait()
        full[rnd, core] = half[rnd] + far[rnd]
        copy = move(2, full.at[rnd, core], full.at[rnd, core], (p, beside))
        copy.start()
        copy.wait()
        top = full[rnd, 0, pl.ds(0, 128), :]
        mid = jnp.concatenate([full[rnd, 0, pl.ds(128, 64), :], full[rnd, 1, pl.ds(0, 64), :]], axis=0)
        low = full[rnd, 1, pl.ds(64, 128), :]
        return jnp.concatenate(
            [jnp.concatenate([top, mid], axis=1), jnp.concatenate([mid.T, low], axis=1)], axis=0
        )

    def off_mass(gram):
        row = lax.broadcasted_iota(jnp.int32, (WIDE, WIDE), 0)
        col = lax.broadcasted_iota(jnp.int32, (WIDE, WIDE), 1)
        squares = jnp.where(row == col, 0.0, gram * gram)
        return jnp.sum(jnp.sum(squares, axis=1, keepdims=True), axis=0, keepdims=True)

    def take_turn(gram):
        turn = rotation(gram * gram_scale, s, splat)
        high, low = halves(turn)
        qh[...] = high
        ql[...] = low
        return turn

    def turned(x, qh=qh, ql=ql):
        high, low = halves(x)
        return bdot(low, qh[...], 1, 0) + bdot(high, ql[...], 1, 0) + bdot(high, qh[...], 1, 0)

    def chunk(c):
        return c, rows(c)

    def small_chunk(v):
        return chunks_a + v, pl.ds(pl.multiple_of(rows_a + v * SMALL, SMALL), SMALL)

    def up(c):
        src, dst = sent.at[up_from, c[1]], got.at[0, c[1]]
        return remote(src, dst, up_s.at[c[0]], up_r.at[c[0]], (p + 1, r))

    def down(c):
        src, dst = sent.at[1, c[1]], got.at[1, c[1]]
        return remote(src, dst, dn_s.at[c[0]], dn_r.at[c[0]], (p - 1, r))

    def raw_copy(i):
        at = pl.ds(0, RAW_FIRST) if i == 0 else pl.ds(RAW_FIRST, RAW * CHUNK - RAW_FIRST)
        return remote(a_ref.at[at], raw.at[at], raw_s.at[i], raw_r.at[i], (mate, r))

    def relay(c):
        return remote(relayed.at[rows(c)], got.at[odd, rows(c)], rel_s.at[c], rel_r.at[c], (to, r))

    def turn_copy(step):
        if step == 0:
            return remote(q_out.at[core], q_in.at[core], turn_s.at[0], turn_r.at[0], (mate, r))
        return remote(q_in.at[core], q_in.at[core], turn_s.at[1], turn_r.at[1], (p, beside))

    def send(c):
        @pl.when(has_up)
        def _():
            up(c).start()

        @pl.when(has_dn)
        def _():
            down(c).start()

    def receive(c):
        @pl.when(has_dn)
        def _():
            up(c).wait_recv()

        @pl.when(has_up)
        def _():
            down(c).wait_recv()

    def keep_ends(at, y):
        @pl.when(p == 0)
        def _():
            got[0, at, :] = y[:, :BLK]

        @pl.when(p == pairs - 1)
        def _():
            got[1, at, :] = y[:, :BLK]

    def turn_rows(at):
        y = turned(held[at, :])
        sent[0, at, :] = y[:, :BLK]
        sent[1, at, :] = y[:, BLK:]
        keep_ends(at, y)

    def arrived(at):
        return jnp.concatenate([got[0, at, :], got[1, at, :]], axis=1)

    def group_copy(stage, k):
        here = place[stage]
        other = lax.rem(here + k, sizes[stage])
        dst = groups.at[stage, here]
        return remote(mine.at[stage], dst, grp_s.at[stage, k], grp_r.at[stage, here], group_device(stage, other))

    def group_send(stage, value):
        mine[stage] = value
        groups[stage, place[stage]] = value
        for k in range(1, sizes[stage]):
            group_copy(stage, k).start()

    def group_sum(stage):
        for k in range(1, sizes[stage]):
            other = lax.rem(place[stage] + k, sizes[stage])
            dst = groups.at[stage, other]
            remote(
                mine.at[stage], dst, grp_s.at[stage, k], grp_r.at[stage, other], group_device(stage, other)
            ).wait_recv()
        total = groups[stage, 0]
        for other in range(1, sizes[stage]):
            total = total + groups[stage, other]
        return total

    clear_gram()
    for i in range(pieces):
        load(i).wait()
        if i == pieces // 2:
            barrier()
            raw_copy(0).start()
        add_gram(held[rows(i, PIECE), :])

    def rest_of_raw():
        raw_copy(1).start()

    gram = sum_over_row(0, rest_of_raw)
    mass_one = off_mass(gram)
    turn = take_turn(gram)
    q_out[0] = turn[:BLK]
    q_out[1] = turn[BLK:]
    turn_copy(0).start()

    @pl.loop(RAW, chunks_a)
    def _(c):
        turn_rows(rows(c))
        send(chunk(c))

    turn_copy(0).wait_recv()
    turn_copy(1).start()
    turn_copy(1).wait()
    for i in range(2):
        high, low = halves(q_in[i])
        ph[pl.ds(i * BLK, BLK), :] = high
        pl_[pl.ds(i * BLK, BLK), :] = low

    raw_copy(0).wait_recv()
    raw_copy(1).wait_recv()

    @pl.loop(0, RAW)
    def _(c):
        y = turned(raw[rows(c), :], ph, pl_)
        top, bottom = y[:, :BLK], y[:, BLK:]
        got[1 - odd, rows(c), :] = jnp.where((odd == 0) | (p == 1), bottom, top)
        relayed[rows(c), :] = jnp.where(odd == 0, top, bottom)

        @pl.when(has_to)
        def _():
            relay(c).start()

        @pl.when((p == 0) | (p == pairs - 1))
        def _():
            keep_ends(rows(c), turned(held[rows(c), :]))

    load(pieces).wait()

    @pl.loop(0, rows_v // PIECE)
    def _(c):
        turn_rows(pl.ds(pl.multiple_of(rows_a + c * PIECE, PIECE), PIECE))

    for v in range(EARLY):
        send(small_chunk(v))

    clear_gram()

    @pl.loop(0, RAW)
    def _(c):
        @pl.when(has_source)
        def _():
            relay(c).wait_recv()

        add_gram(arrived(rows(c)))

    @pl.loop(RAW, chunks_a)
    def _(c):
        receive(chunk(c))
        add_gram(arrived(rows(c)))

    def some_vectors():
        for v in range(EARLY, EARLY + MIDDLE):
            send(small_chunk(v))

    gram = sum_over_row(1, some_vectors)
    mass_two = off_mass(gram)
    first = lax.broadcasted_iota(jnp.int32, (8, 128), 1) == 0
    both = jnp.where(first, jnp.broadcast_to(mass_one, (8, 128)), jnp.broadcast_to(mass_two, (8, 128)))
    group_send(0, both)

    @pl.loop(EARLY + MIDDLE, small)
    def _(v):
        send(small_chunk(v))

    take_turn(gram)
    group_send(1, group_sum(0))

    pieces_v = rows_v // SMALL

    def out(c):
        return pltpu.make_async_copy(done.at[rows(c, PIECE)], ao_ref.at[rows(c, PIECE)], out_sem.at[c])

    def out_v(v):
        return pltpu.make_async_copy(done.at[small_chunk(v)[1]], vo_ref.at[rows(v, SMALL)], out_sem.at[pieces + v])

    @pl.loop(0, pieces)
    def _(c):
        done[rows(c, PIECE), :] = turned(arrived(rows(c, PIECE)))
        out(c).start()

    @pl.loop(0, pieces_v)
    def _(v):
        receive(small_chunk(v))
        at = small_chunk(v)[1]
        done[at, :] = turned(arrived(at))
        out_v(v).start()

    m_ref[...] = group_sum(1) * mass_scale

    def sent_all(c):
        @pl.when(has_up)
        def _():
            up(c).wait_send()

        @pl.when(has_dn)
        def _():
            down(c).wait_send()

    @pl.loop(RAW, chunks_a)
    def _(c):
        sent_all(chunk(c))

    @pl.loop(0, small)
    def _(v):
        sent_all(small_chunk(v))

    raw_copy(0).wait_send()
    raw_copy(1).wait_send()

    @pl.loop(0, RAW)
    def _(c):
        @pl.when(has_to)
        def _():
            relay(c).wait_send()

    turn_copy(0).wait_send()
    for stage in range(2):
        for k in range(1, sizes[stage]):
            group_copy(stage, k).wait_send()

    @pl.loop(0, pieces)
    def _(c):
        out(c).wait()

    @pl.loop(0, pieces_v)
    def _(v):
        out_v(v).wait()


def local(pairs, matrix, vectors):
    rows_a, rows_v = matrix.shape[0], vectors.shape[0]
    total_rows = float(rows_a * lax.axis_size("row"))
    sends = rows_a // CHUNK + rows_v // SMALL
    body = functools.partial(kernel, pairs, 2.0**-13, 1.0 / (total_rows * total_rows * float(pairs)))
    dma = pltpu.SemaphoreType.DMA
    vmem = pltpu.VMEM
    matrix_out, vectors_out, mass = pl.pallas_call(
        body,
        out_shape=(
            jax.ShapeDtypeStruct(matrix.shape, F32),
            jax.ShapeDtypeStruct(vectors.shape, F32),
            jax.ShapeDtypeStruct((8, 128), F32),
        ),
        in_specs=[pl.BlockSpec(memory_space=pltpu.HBM)] * 2,
        out_specs=(
            pl.BlockSpec(memory_space=pl.ANY),
            pl.BlockSpec(memory_space=pl.ANY),
            pl.BlockSpec(memory_space=vmem),
        ),
        scratch_shapes=[
            vmem((rows_a + rows_v, WIDE), F32),
            vmem((2, rows_a + rows_v, BLK), F32),
            vmem((2, rows_a + rows_v, BLK), F32),
            vmem((rows_a + rows_v, WIDE), F32),
            vmem((RAW * CHUNK, WIDE), F32),
            vmem((RAW * CHUNK, BLK), F32),
            vmem((WIDE, WIDE), F32),
            vmem((8, 8, 128), F32),
            vmem((WIDE, WIDE), F32),
            vmem((WIDE, WIDE), F32),
            vmem((WIDE, WIDE), jnp.bfloat16),
            vmem((WIDE, WIDE), jnp.bfloat16),
            vmem((WIDE, WIDE), jnp.bfloat16),
            vmem((WIDE, WIDE), jnp.bfloat16),
            vmem((2, BLK, WIDE), F32),
            vmem((2, BLK, WIDE), F32),
            vmem((2, 2, 192, 128), F32),
            vmem((2, 192, 128), F32),
            vmem((2, 192, 128), F32),
            vmem((2, 192, 128), F32),
            vmem((2, 2, 192, 128), F32),
            vmem((2, 8, 128), F32),
            vmem((2, 8, 8, 128), F32),
            dma((rows_a // PIECE + 1,)),
            dma((sends,)),
            dma((sends,)),
            dma((sends,)),
            dma((sends,)),
            dma((2,)),
            dma((2,)),
            dma((RAW,)),
            dma((RAW,)),
            dma((2,)),
            dma((2,)),
            dma((2, 3)),
            dma((2, 3)),
            dma((2, 8)),
            dma((2, 8)),
            dma((rows_a // PIECE + rows_v // SMALL,)),
        ],
        compiler_params=pltpu.CompilerParams(
            collective_id=0, has_side_effects=True, vmem_limit_bytes=40 * 2**20
        ),
    )(matrix, vectors)
    return matrix_out, vectors_out, mass[0, :2]


def solution(mesh):
    return jax.shard_map(
        functools.partial(local, mesh.shape["pair"]),
        mesh=mesh,
        in_specs=(P("row", "pair"), P("row", "pair")),
        out_specs=(P("row", "pair"), P("row", "pair"), P()),
        check_vma=False,
    )
```

```python
import functools

import jax
import jax.numpy as jnp
from jax import lax
from jax.experimental import pallas as pl
from jax.experimental.pallas import tpu as pltpu
from jax.sharding import PartitionSpec as P

HIGH = lax.Precision.HIGHEST
MESH = pl.DeviceIdType.MESH
F32 = jnp.float32
BLK = 128
WIDE = 2 * BLK
OUTER = 32
PIECE = 512
CHUNK = 256
SMALL = 128
RAW = 3
RAW_FIRST = 128
EARLY = 2
MIDDLE = 1
CORRECT = 1


def dot(a, b, ca, cb):
    dims = (((ca,), (cb,)), ((), ()))
    return lax.dot_general(a, b, dims, precision=HIGH, preferred_element_type=F32)


def bdot(a, b, ca, cb):
    dims = (((ca,), (cb,)), ((), ()))
    return lax.dot_general(a, b, dims, preferred_element_type=F32)


def halves(a):
    high = a.astype(jnp.bfloat16)
    return high, (a - high.astype(F32)).astype(jnp.bfloat16)


def dot3(a, b, ca, cb):
    ah, al = halves(a)
    bh, bl = halves(b)
    return bdot(al, bh, ca, cb) + bdot(ah, bl, ca, cb) + bdot(ah, bh, ca, cb)


def wide(v):
    return jnp.concatenate([v] * (WIDE // 128), axis=1)


def panel(s, splat, k, end):
    c0 = (k // 128) * 128
    own = s[pl.ds(k, 8), pl.ds(c0, 128)]
    for j in range(8):
        at = k - c0 + j
        splat[j] = jnp.broadcast_to(own[:, at : at + 1], (8, 128))
    e = {(i, j): splat[j, i : i + 1, :] for j in range(8) for i in range(j, 8)}
    lanes = lax.broadcasted_iota(jnp.int32, (1, WIDE), 1)
    rows = []
    for i in range(8):
        row = s[pl.ds(k + i, 1), :]
        row = jnp.where((lanes >= k) & (lanes < k + 8), 0.0, row)
        rows.append(jnp.where(lanes == k + i, 1.0, row))
    l = {}
    scale = []
    for a in range(0, 8, 2):
        b = a + 1
        p, q, t = e[a, a], e[b, a], e[b, b]
        ra, rd = lax.rsqrt(p), lax.rsqrt(p * t - q * q)
        rb = rd * (p * ra)
        scale += [ra, rb]
        l[b, a] = q * ra
        for i in range(b + 1, 8):
            l[i, a] = e[i, a] * ra
            l[i, b] = (e[i, b] - l[i, a] * l[b, a]) * rb
        for j in range(b + 1, 8):
            for i in range(j, 8):
                e[i, j] = e[i, j] - (l[i, a] * l[j, a] + l[i, b] * l[j, b])
        rows[a] = rows[a] * wide(ra)
        rows[b] = (rows[b] - wide(l[b, a]) * rows[a]) * wide(rb)
        for i in range(b + 1, 8):
            rows[i] = rows[i] - (wide(l[i, a]) * rows[a] + wide(l[i, b]) * rows[b])
    for i in range(8):
        s[pl.ds(k + i, 1), :] = rows[i]
    full = [jnp.broadcast_to(row, (8, WIDE)) for row in rows]
    lanes = lax.broadcasted_iota(jnp.int32, (8, WIDE), 1)
    inside = (lanes >= k) & (lanes < k + 8)
    for g in range(k + 8, end, 8):
        old = s[pl.ds(g, 8), :]
        m = []
        for j in range(8):
            at = k + j
            t = jnp.broadcast_to(old[:, at : at + 1], (8, 128))
            for jj in range(j):
                t = t - m[jj] * jnp.broadcast_to(l[j, jj], (8, 128))
            m.append(t * jnp.broadcast_to(scale[j], (8, 128)))
        new = jnp.where(inside, 0.0, old)
        for j in range(8):
            new = new - wide(m[j]) * full[j]
        s[pl.ds(g, 8), :] = new


def factor_inverse(s, splat):
    for b0 in range(0, WIDE, OUTER):
        b1 = b0 + OUTER
        for k in range(b0, b1, 8):
            panel(s, splat, k, b1)
        if b1 == WIDE:
            break
        lanes = lax.broadcasted_iota(jnp.int32, (OUTER, WIDE), 1)
        row = lax.broadcasted_iota(jnp.int32, (OUTER, WIDE), 0)
        block = jnp.where((lanes < b1) & (lanes > row + b0), 0.0, s[pl.ds(b0, OUTER), :])
        rest = s[pl.ds(b1, WIDE - b1), :]
        c0 = (b0 // 128) * 128
        near = lax.broadcasted_iota(jnp.int32, (1, 128), 1) + c0
        inverse = jnp.where((near >= b0) & (near < b1), block[:, c0 : c0 + 128], 0.0)
        factor = dot3(rest[:, c0 : c0 + 128], inverse, 1, 1)
        lanes = lax.broadcasted_iota(jnp.int32, (1, WIDE), 1)
        rest = jnp.where((lanes >= b0) & (lanes < b1), 0.0, rest)
        s[pl.ds(b1, WIDE - b1), :] = rest - dot3(factor, block, 1, 0)


def rotation(gram, s, splat):
    square = dot(gram, gram, 1, 0)
    s[...] = dot(square, square, 1, 0)
    factor_inverse(s, splat)
    row = lax.broadcasted_iota(jnp.int32, (WIDE, WIDE), 0)
    col = lax.broadcasted_iota(jnp.int32, (WIDE, WIDE), 1)
    turn = dot(square, jnp.where(row >= col, s[...], 0.0), 1, 1)
    for _ in range(CORRECT):
        over = dot(turn, turn, 0, 0)
        over = jnp.where(row == col, (over - 1.0) * 0.5, jnp.where(row < col, over, 0.0))
        turn = turn - dot(turn, over, 1, 0)
    return turn


def kernel(
    pairs, gram_scale, mass_scale,
    a_ref, v_ref, ao_ref, vo_ref, m_ref,
    held, sent, got, done, raw, relayed, s, splat, hh, hl, qh, ql, ph, pl_, q_out, q_in,
    part, near, half, far, full, mine, groups,
    answer, group_answer, in_sem, up_s, up_r, dn_s, dn_r, raw_s, raw_r, rel_s, rel_r, turn_s, turn_r, sum_s, sum_r, grp_s, grp_r, out_sem,
):
    rows_a, rows_v = a_ref.shape[0], v_ref.shape[0]
    chunks_a, small = rows_a // CHUNK, rows_v // SMALL
    inner = min(8, pairs)
    outer = pairs // inner
    p, r = lax.axis_index("pair"), lax.axis_index("row")
    core = lax.rem(r, 2)
    beside = r + 1 - 2 * core
    across = lax.rem(r + 2, 4)
    odd = lax.rem(p, 2)
    mate = p + 1 - 2 * odd
    to = p + 2 - 4 * odd
    source = p - 2 + 4 * odd
    beyond = p - 1 + 2 * odd
    pa, pb = p // inner, lax.rem(p, inner)
    halves_z = 2 - outer % 2
    count_y = outer // halves_z
    pm = lax.rem(pa, halves_z) * count_y + pa // halves_z
    line = inner * halves_z
    up_from = (pairs - p) // pairs
    has_up, has_dn = p < pairs - 1, p > 0
    has_to = (to >= 0) & (to < pairs)
    has_source = (source >= 0) & (source < pairs)
    has_beyond = (beyond >= 0) & (beyond < pairs)
    last_of_line = (lax.rem(p, line) == line - 1) & (p < pairs - 1)

    def group_device(stage, other):
        if stage == 0:
            return (pa * inner + other, r)
        return ((lax.rem(other, count_y) * halves_z + other // count_y) * inner + pb, r)

    sizes, place = (inner, outer), (pb, pm)

    def later(other):
        return (other > p) == (other // line == p // line)

    def remote(src, dst, send_sem, recv_sem, device):
        return pltpu.make_async_remote_copy(
            src_ref=src, dst_ref=dst, send_sem=send_sem, recv_sem=recv_sem, device_id=device, device_id_type=MESH
        )

    bar = pltpu.get_barrier_semaphore()

    def hello(device):
        pl.semaphore_signal(bar, 1, device_id=device, device_id_type=MESH)

    hello((p, beside))
    hello((p, across))
    hello((mate, r))
    others = ((has_beyond, beyond, 0), (has_to, to, 2), (has_source, source, 1))
    for there, device, _ in others:

        @pl.when(there & later(device))
        def _(device=device):
            hello((device, r))

    def group_peers():
        for stage in range(2):
            for k in range(1, sizes[stage]):
                yield stage, lax.rem(place[stage] + k, sizes[stage])

    for stage, other in group_peers():

        @pl.when(other > place[stage])
        def _(stage=stage, other=other):
            hello(group_device(stage, other))

    def barrier():
        count = 3 + pb + pm
        for there, device, _ in others:
            count = count + jnp.where(there & jnp.logical_not(later(device)), 1, 0)
        pl.semaphore_wait(bar, count)
        for there, device, which in others:

            @pl.when(there & jnp.logical_not(later(device)))
            def _(device=device, which=which):
                pl.semaphore_signal(answer.at[which], 1, device_id=(device, r), device_id_type=MESH)

        for stage, other in group_peers():

            @pl.when(other < place[stage])
            def _(stage=stage, other=other):
                device = group_device(stage, other)
                pl.semaphore_signal(group_answer.at[stage], 1, device_id=device, device_id_type=MESH)

    def answered(which):
        there, device, _ = others[which]

        @pl.when(there & later(device))
        def _():
            pl.semaphore_wait(answer.at[which], 1)

    def group_answered(stage):
        @pl.when(place[stage] < sizes[stage] - 1)
        def _():
            pl.semaphore_wait(group_answer.at[stage], sizes[stage] - 1 - place[stage])

    def rows(c, size=CHUNK):
        return pl.ds(pl.multiple_of(c * size, size), size)

    pieces = rows_a // PIECE

    def load(i):
        src = a_ref.at[rows(i, PIECE)] if i < pieces else v_ref
        size = PIECE if i < pieces else rows_v
        return pltpu.make_async_copy(src, held.at[pl.ds(i * PIECE, size)], in_sem.at[i])

    for i in range(pieces + 1):
        load(i).start()

    def add_gram(x):
        high, low = halves(x)
        hh[...] += bdot(high, high, 0, 0)
        hl[...] += bdot(high, low, 0, 0)

    def clear_gram():
        hh[...] = jnp.zeros_like(hh)
        hl[...] = jnp.zeros_like(hl)

    def sum_over_row(rnd, between):
        cross = hl[...]
        gram = hh[...] + (cross + cross.T)
        part[rnd, 0, pl.ds(0, 128), :] = gram[:128, :128]
        part[rnd, 0, pl.ds(128, 64), :] = gram[:64, 128:]
        part[rnd, 1, pl.ds(0, 64), :] = gram[64:128, 128:]
        part[rnd, 1, pl.ds(64, 128), :] = gram[128:, 128:]

        def move(step, src, dst, device):
            return remote(src, dst, sum_s.at[rnd, step], sum_r.at[rnd, step], device)

        copy = move(0, part.at[rnd, 1 - core], near.at[rnd], (p, beside))
        copy.start()
        copy.wait()
        half[rnd] = part[rnd, core] + near[rnd]
        copy = move(1, half.at[rnd], far.at[rnd], (p, across))
        copy.start()
        between()
        copy.wait()
        full[rnd, core] = half[rnd] + far[rnd]
        copy = move(2, full.at[rnd, core], full.at[rnd, core], (p, beside))
        copy.start()
        copy.wait()
        top = full[rnd, 0, pl.ds(0, 128), :]
        mid = jnp.concatenate([full[rnd, 0, pl.ds(128, 64), :], full[rnd, 1, pl.ds(0, 64), :]], axis=0)
        low = full[rnd, 1, pl.ds(64, 128), :]
        return jnp.concatenate(
            [jnp.concatenate([top, mid], axis=1), jnp.concatenate([mid.T, low], axis=1)], axis=0
        )

    def off_mass(gram):
        row = lax.broadcasted_iota(jnp.int32, (WIDE, WIDE), 0)
        col = lax.broadcasted_iota(jnp.int32, (WIDE, WIDE), 1)
        squares = jnp.where(row == col, 0.0, gram * gram)
        return jnp.sum(jnp.sum(squares, axis=1, keepdims=True), axis=0, keepdims=True)

    def take_turn(gram):
        turn = rotation(gram * gram_scale, s, splat)
        high, low = halves(turn)
        qh[...] = high
        ql[...] = low
        return turn

    def turned(x, qh=qh, ql=ql):
        high, low = halves(x)
        return bdot(low, qh[...], 1, 0) + bdot(high, ql[...], 1, 0) + bdot(high, qh[...], 1, 0)

    def chunk(c):
        return c, rows(c)

    def small_chunk(v):
        return chunks_a + v, pl.ds(pl.multiple_of(rows_a + v * SMALL, SMALL), SMALL)

    def up(c):
        src, dst = sent.at[up_from, c[1]], got.at[0, c[1]]
        return remote(src, dst, up_s.at[c[0]], up_r.at[c[0]], (p + 1, r))

    def down(c):
        src, dst = sent.at[1, c[1]], got.at[1, c[1]]
        return remote(src, dst, dn_s.at[c[0]], dn_r.at[c[0]], (p - 1, r))

    def raw_copy(i):
        at = pl.ds(0, RAW_FIRST) if i == 0 else pl.ds(RAW_FIRST, RAW * CHUNK - RAW_FIRST)
        return remote(a_ref.at[at], raw.at[at], raw_s.at[i], raw_r.at[i], (mate, r))

    def relay(c):
        return remote(relayed.at[rows(c)], got.at[odd, rows(c)], rel_s.at[c], rel_r.at[c], (to, r))

    def turn_copy(step):
        if step == 0:
            return remote(q_out.at[core], q_in.at[core], turn_s.at[0], turn_r.at[0], (mate, r))
        return remote(q_in.at[core], q_in.at[core], turn_s.at[1], turn_r.at[1], (p, beside))

    def send_up(c):
        @pl.when(has_up)
        def _():
            up(c).start()

    def send_down(c):
        @pl.when(has_dn)
        def _():
            down(c).start()

    def send_all(lo, hi, make, before=lambda c: None):
        @pl.loop(lo, hi)
        def _(c):
            before(c)
            send_up(make(c))

            @pl.when(jnp.logical_not(last_of_line))
            def _():
                send_down(make(c))

        @pl.when(last_of_line)
        def _():
            @pl.loop(lo, hi)
            def _(c):
                send_down(make(c))

    def receive(c):
        @pl.when(has_dn)
        def _():
            up(c).wait_recv()

        @pl.when(has_up)
        def _():
            down(c).wait_recv()

    def keep_ends(at, y):
        @pl.when(p == 0)
        def _():
            got[0, at, :] = y[:, :BLK]

        @pl.when(p == pairs - 1)
        def _():
            got[1, at, :] = y[:, :BLK]

    def turn_rows(at):
        y = turned(held[at, :])
        sent[0, at, :] = y[:, :BLK]
        sent[1, at, :] = y[:, BLK:]
        keep_ends(at, y)

    def arrived(at):
        return jnp.concatenate([got[0, at, :], got[1, at, :]], axis=1)

    def group_copy(stage, k):
        here = place[stage]
        other = lax.rem(here + k, sizes[stage])
        dst = groups.at[stage, here]
        return remote(mine.at[stage], dst, grp_s.at[stage, k], grp_r.at[stage, here], group_device(stage, other))

    def group_send(stage, value):
        group_answered(stage)
        mine[stage] = value
        groups[stage, place[stage]] = value
        for k in range(1, sizes[stage]):
            group_copy(stage, k).start()

    def group_sum(stage):
        for k in range(1, sizes[stage]):
            other = lax.rem(place[stage] + k, sizes[stage])
            dst = groups.at[stage, other]
            remote(
                mine.at[stage], dst, grp_s.at[stage, k], grp_r.at[stage, other], group_device(stage, other)
            ).wait_recv()
        total = groups[stage, 0]
        for other in range(1, sizes[stage]):
            total = total + groups[stage, other]
        return total

    clear_gram()
    for i in range(pieces):
        load(i).wait()
        if i == pieces // 2:
            barrier()
            raw_copy(0).start()
        add_gram(held[rows(i, PIECE), :])

    def rest_of_raw():
        raw_copy(1).start()

    gram = sum_over_row(0, rest_of_raw)
    mass_one = off_mass(gram)
    turn = take_turn(gram)
    q_out[0] = turn[:BLK]
    q_out[1] = turn[BLK:]
    turn_copy(0).start()

    answered(0)
    send_all(RAW, chunks_a, chunk, lambda c: turn_rows(rows(c)))

    turn_copy(0).wait_recv()
    turn_copy(1).start()
    turn_copy(1).wait()
    for i in range(2):
        high, low = halves(q_in[i])
        ph[pl.ds(i * BLK, BLK), :] = high
        pl_[pl.ds(i * BLK, BLK), :] = low

    raw_copy(0).wait_recv()
    raw_copy(1).wait_recv()
    answered(1)
    answered(2)

    @pl.loop(0, RAW)
    def _(c):
        y = turned(raw[rows(c), :], ph, pl_)
        top, bottom = y[:, :BLK], y[:, BLK:]
        got[1 - odd, rows(c), :] = jnp.where((odd == 0) | (p == 1), bottom, top)
        relayed[rows(c), :] = jnp.where(odd == 0, top, bottom)

        @pl.when(has_to)
        def _():
            relay(c).start()

        @pl.when((p == 0) | (p == pairs - 1))
        def _():
            keep_ends(rows(c), turned(held[rows(c), :]))

    load(pieces).wait()

    @pl.loop(0, rows_v // PIECE)
    def _(c):
        turn_rows(pl.ds(pl.multiple_of(rows_a + c * PIECE, PIECE), PIECE))

    send_all(0, EARLY, small_chunk)

    clear_gram()

    @pl.loop(0, RAW)
    def _(c):
        @pl.when(has_source)
        def _():
            relay(c).wait_recv()

        add_gram(arrived(rows(c)))

    @pl.loop(RAW, chunks_a)
    def _(c):
        receive(chunk(c))
        add_gram(arrived(rows(c)))

    def some_vectors():
        send_all(EARLY, EARLY + MIDDLE, small_chunk)

    gram = sum_over_row(1, some_vectors)
    mass_two = off_mass(gram)
    first = lax.broadcasted_iota(jnp.int32, (8, 128), 1) == 0
    both = jnp.where(first, jnp.broadcast_to(mass_one, (8, 128)), jnp.broadcast_to(mass_two, (8, 128)))
    group_send(0, both)

    send_all(EARLY + MIDDLE, small, small_chunk)

    take_turn(gram)
    group_send(1, group_sum(0))

    pieces_v = rows_v // SMALL

    def out(c):
        return pltpu.make_async_copy(done.at[rows(c, PIECE)], ao_ref.at[rows(c, PIECE)], out_sem.at[c])

    def out_v(v):
        return pltpu.make_async_copy(done.at[small_chunk(v)[1]], vo_ref.at[rows(v, SMALL)], out_sem.at[pieces + v])

    @pl.loop(0, pieces)
    def _(c):
        done[rows(c, PIECE), :] = turned(arrived(rows(c, PIECE)))
        out(c).start()

    @pl.loop(0, pieces_v)
    def _(v):
        receive(small_chunk(v))
        at = small_chunk(v)[1]
        done[at, :] = turned(arrived(at))
        out_v(v).start()

    m_ref[...] = group_sum(1) * mass_scale

    def sent_all(c):
        @pl.when(has_up)
        def _():
            up(c).wait_send()

        @pl.when(has_dn)
        def _():
            down(c).wait_send()

    @pl.loop(RAW, chunks_a)
    def _(c):
        sent_all(chunk(c))

    @pl.loop(0, small)
    def _(v):
        sent_all(small_chunk(v))

    raw_copy(0).wait_send()
    raw_copy(1).wait_send()

    @pl.loop(0, RAW)
    def _(c):
        @pl.when(has_to)
        def _():
            relay(c).wait_send()

    turn_copy(0).wait_send()
    for stage in range(2):
        for k in range(1, sizes[stage]):
            group_copy(stage, k).wait_send()

    @pl.loop(0, pieces)
    def _(c):
        out(c).wait()

    @pl.loop(0, pieces_v)
    def _(v):
        out_v(v).wait()


def local(pairs, matrix, vectors):
    rows_a, rows_v = matrix.shape[0], vectors.shape[0]
    total_rows = float(rows_a * lax.axis_size("row"))
    sends = rows_a // CHUNK + rows_v // SMALL
    body = functools.partial(kernel, pairs, 2.0**-13, 1.0 / (total_rows * total_rows * float(pairs)))
    dma = pltpu.SemaphoreType.DMA
    vmem = pltpu.VMEM
    matrix_out, vectors_out, mass = pl.pallas_call(
        body,
        out_shape=(
            jax.ShapeDtypeStruct(matrix.shape, F32),
            jax.ShapeDtypeStruct(vectors.shape, F32),
            jax.ShapeDtypeStruct((8, 128), F32),
        ),
        in_specs=[pl.BlockSpec(memory_space=pltpu.HBM)] * 2,
        out_specs=(
            pl.BlockSpec(memory_space=pl.ANY),
            pl.BlockSpec(memory_space=pl.ANY),
            pl.BlockSpec(memory_space=vmem),
        ),
        scratch_shapes=[
            vmem((rows_a + rows_v, WIDE), F32),
            vmem((2, rows_a + rows_v, BLK), F32),
            vmem((2, rows_a + rows_v, BLK), F32),
            vmem((rows_a + rows_v, WIDE), F32),
            vmem((RAW * CHUNK, WIDE), F32),
            vmem((RAW * CHUNK, BLK), F32),
            vmem((WIDE, WIDE), F32),
            vmem((8, 8, 128), F32),
            vmem((WIDE, WIDE), F32),
            vmem((WIDE, WIDE), F32),
            vmem((WIDE, WIDE), jnp.bfloat16),
            vmem((WIDE, WIDE), jnp.bfloat16),
            vmem((WIDE, WIDE), jnp.bfloat16),
            vmem((WIDE, WIDE), jnp.bfloat16),
            vmem((2, BLK, WIDE), F32),
            vmem((2, BLK, WIDE), F32),
            vmem((2, 2, 192, 128), F32),
            vmem((2, 192, 128), F32),
            vmem((2, 192, 128), F32),
            vmem((2, 192, 128), F32),
            vmem((2, 2, 192, 128), F32),
            vmem((2, 8, 128), F32),
            vmem((2, 8, 8, 128), F32),
            pltpu.SemaphoreType.REGULAR((3,)),
            pltpu.SemaphoreType.REGULAR((2,)),
            dma((rows_a // PIECE + 1,)),
            dma((sends,)),
            dma((sends,)),
            dma((sends,)),
            dma((sends,)),
            dma((2,)),
            dma((2,)),
            dma((RAW,)),
            dma((RAW,)),
            dma((2,)),
            dma((2,)),
            dma((2, 3)),
            dma((2, 3)),
            dma((2, 8)),
            dma((2, 8)),
            dma((rows_a // PIECE + rows_v // SMALL,)),
        ],
        compiler_params=pltpu.CompilerParams(
            collective_id=0, has_side_effects=True, vmem_limit_bytes=40 * 2**20
        ),
    )(matrix, vectors)
    return matrix_out, vectors_out, mass[0, :2]


def solution(mesh):
    return jax.shard_map(
        functools.partial(local, mesh.shape["pair"]),
        mesh=mesh,
        in_specs=(P("row", "pair"), P("row", "pair")),
        out_specs=(P("row", "pair"), P("row", "pair"), P()),
        check_vma=False,
    )
```

```python
import functools

import jax
import jax.numpy as jnp
from jax import lax
from jax.experimental import pallas as pl
from jax.experimental.pallas import tpu as pltpu
from jax.sharding import PartitionSpec as P

HIGH = lax.Precision.HIGHEST
MESH = pl.DeviceIdType.MESH
F32 = jnp.float32
BLK = 128
WIDE = 2 * BLK
OUTER = 32
PIECE = 512
CHUNK = 256
SMALL = 128
RAW = 3
RAW_FIRST = 128
EARLY = 2
MIDDLE = 1
CORRECT = 1


def dot(a, b, ca, cb):
    dims = (((ca,), (cb,)), ((), ()))
    return lax.dot_general(a, b, dims, precision=HIGH, preferred_element_type=F32)


def bdot(a, b, ca, cb):
    dims = (((ca,), (cb,)), ((), ()))
    return lax.dot_general(a, b, dims, preferred_element_type=F32)


def halves(a):
    high = a.astype(jnp.bfloat16)
    return high, (a - high.astype(F32)).astype(jnp.bfloat16)


def dot3(a, b, ca, cb):
    ah, al = halves(a)
    bh, bl = halves(b)
    return bdot(al, bh, ca, cb) + bdot(ah, bl, ca, cb) + bdot(ah, bh, ca, cb)


def wide(v):
    return jnp.concatenate([v] * (WIDE // 128), axis=1)


def panel(s, splat, k, end):
    c0 = (k // 128) * 128
    own = s[pl.ds(k, 8), pl.ds(c0, 128)]
    for j in range(8):
        at = k - c0 + j
        splat[j] = jnp.broadcast_to(own[:, at : at + 1], (8, 128))
    e = {(i, j): splat[j, i : i + 1, :] for j in range(8) for i in range(j, 8)}
    lanes = lax.broadcasted_iota(jnp.int32, (1, WIDE), 1)
    rows = []
    for i in range(8):
        row = s[pl.ds(k + i, 1), :]
        row = jnp.where((lanes >= k) & (lanes < k + 8), 0.0, row)
        rows.append(jnp.where(lanes == k + i, 1.0, row))
    l = {}
    scale = []
    for a in range(0, 8, 2):
        b = a + 1
        p, q, t = e[a, a], e[b, a], e[b, b]
        ra, rd = lax.rsqrt(p), lax.rsqrt(p * t - q * q)
        rb = rd * (p * ra)
        scale += [ra, rb]
        l[b, a] = q * ra
        for i in range(b + 1, 8):
            l[i, a] = e[i, a] * ra
            l[i, b] = (e[i, b] - l[i, a] * l[b, a]) * rb
        for j in range(b + 1, 8):
            for i in range(j, 8):
                e[i, j] = e[i, j] - (l[i, a] * l[j, a] + l[i, b] * l[j, b])
        rows[a] = rows[a] * wide(ra)
        rows[b] = (rows[b] - wide(l[b, a]) * rows[a]) * wide(rb)
        for i in range(b + 1, 8):
            rows[i] = rows[i] - (wide(l[i, a]) * rows[a] + wide(l[i, b]) * rows[b])
    for i in range(8):
        s[pl.ds(k + i, 1), :] = rows[i]
    full = [jnp.broadcast_to(row, (8, WIDE)) for row in rows]
    lanes = lax.broadcasted_iota(jnp.int32, (8, WIDE), 1)
    inside = (lanes >= k) & (lanes < k + 8)
    for g in range(k + 8, end, 8):
        old = s[pl.ds(g, 8), :]
        m = []
        for j in range(8):
            at = k + j
            t = jnp.broadcast_to(old[:, at : at + 1], (8, 128))
            for jj in range(j):
                t = t - m[jj] * jnp.broadcast_to(l[j, jj], (8, 128))
            m.append(t * jnp.broadcast_to(scale[j], (8, 128)))
        new = jnp.where(inside, 0.0, old)
        for j in range(8):
            new = new - wide(m[j]) * full[j]
        s[pl.ds(g, 8), :] = new


def factor_inverse(s, splat):
    for b0 in range(0, WIDE, OUTER):
        b1 = b0 + OUTER
        for k in range(b0, b1, 8):
            panel(s, splat, k, b1)
        if b1 == WIDE:
            break
        lanes = lax.broadcasted_iota(jnp.int32, (OUTER, WIDE), 1)
        row = lax.broadcasted_iota(jnp.int32, (OUTER, WIDE), 0)
        block = jnp.where((lanes < b1) & (lanes > row + b0), 0.0, s[pl.ds(b0, OUTER), :])
        rest = s[pl.ds(b1, WIDE - b1), :]
        c0 = (b0 // 128) * 128
        near = lax.broadcasted_iota(jnp.int32, (1, 128), 1) + c0
        inverse = jnp.where((near >= b0) & (near < b1), block[:, c0 : c0 + 128], 0.0)
        factor = dot3(rest[:, c0 : c0 + 128], inverse, 1, 1)
        lanes = lax.broadcasted_iota(jnp.int32, (1, WIDE), 1)
        rest = jnp.where((lanes >= b0) & (lanes < b1), 0.0, rest)
        s[pl.ds(b1, WIDE - b1), :] = rest - dot3(factor, block, 1, 0)


def rotation(gram, s, splat):
    square = dot(gram, gram, 1, 0)
    s[...] = dot(square, square, 1, 0)
    factor_inverse(s, splat)
    row = lax.broadcasted_iota(jnp.int32, (WIDE, WIDE), 0)
    col = lax.broadcasted_iota(jnp.int32, (WIDE, WIDE), 1)
    turn = dot(square, jnp.where(row >= col, s[...], 0.0), 1, 1)
    for _ in range(CORRECT):
        over = dot(turn, turn, 0, 0)
        over = jnp.where(row == col, (over - 1.0) * 0.5, jnp.where(row < col, over, 0.0))
        turn = turn - dot(turn, over, 1, 0)
    return turn


def kernel(
    pairs, gram_scale, mass_scale,
    a_ref, v_ref, ao_ref, vo_ref, m_ref,
    held, sent, got, done, raw, relayed, s, splat, hh, hl, qh, ql, ph, pl_, q_out, q_in,
    part, near, half, far, full, mine, groups,
    answer, group_answer, in_sem, up_s, up_r, dn_s, dn_r, raw_s, raw_r, rel_s, rel_r, turn_s, turn_r, sum_s, sum_r, grp_s, grp_r, out_sem,
):
    rows_a, rows_v = a_ref.shape[0], v_ref.shape[0]
    chunks_a, small = rows_a // CHUNK, rows_v // SMALL
    inner = min(8, pairs)
    outer = pairs // inner
    p, r = lax.axis_index("pair"), lax.axis_index("row")
    core = lax.rem(r, 2)
    beside = r + 1 - 2 * core
    across = lax.rem(r + 2, 4)
    odd = lax.rem(p, 2)
    mate = p + 1 - 2 * odd
    to = p + 2 - 4 * odd
    source = p - 2 + 4 * odd
    beyond = p - 1 + 2 * odd
    pa, pb = p // inner, lax.rem(p, inner)
    halves_z = 2 - outer % 2
    count_y = outer // halves_z
    pm = lax.rem(pa, halves_z) * count_y + pa // halves_z
    line = inner * halves_z
    up_from = (pairs - p) // pairs
    has_up, has_dn = p < pairs - 1, p > 0
    has_to = (to >= 0) & (to < pairs)
    has_source = (source >= 0) & (source < pairs)
    has_beyond = (beyond >= 0) & (beyond < pairs)
    last_of_line = (lax.rem(p, line) == line - 1) & (p < pairs - 1)

    def group_device(stage, other):
        if stage == 0:
            return (pa * inner + other, r)
        return ((lax.rem(other, count_y) * halves_z + other // count_y) * inner + pb, r)

    sizes, place = (inner, outer), (pb, pm)

    def later(other):
        return (other > p) == (other // line == p // line)

    def remote(src, dst, send_sem, recv_sem, device):
        return pltpu.make_async_remote_copy(
            src_ref=src, dst_ref=dst, send_sem=send_sem, recv_sem=recv_sem, device_id=device, device_id_type=MESH
        )

    bar = pltpu.get_barrier_semaphore()

    def hello(device):
        pl.semaphore_signal(bar, 1, device_id=device, device_id_type=MESH)

    hello((p, beside))
    hello((p, across))
    hello((mate, r))
    others = ((has_beyond, beyond, 0), (has_to, to, 2), (has_source, source, 1))
    for there, device, _ in others:

        @pl.when(there & later(device))
        def _(device=device):
            hello((device, r))

    def group_peers():
        for stage in range(2):
            for k in range(1, sizes[stage]):
                yield stage, lax.rem(place[stage] + k, sizes[stage])

    for stage, other in group_peers():

        @pl.when(other > place[stage])
        def _(stage=stage, other=other):
            hello(group_device(stage, other))

    def barrier():
        count = 3 + pb + pm
        for there, device, _ in others:
            count = count + jnp.where(there & jnp.logical_not(later(device)), 1, 0)
        pl.semaphore_wait(bar, count)
        for there, device, which in others:

            @pl.when(there & jnp.logical_not(later(device)))
            def _(device=device, which=which):
                pl.semaphore_signal(answer.at[which], 1, device_id=(device, r), device_id_type=MESH)

        for stage, other in group_peers():

            @pl.when(other < place[stage])
            def _(stage=stage, other=other):
                device = group_device(stage, other)
                pl.semaphore_signal(group_answer.at[stage], 1, device_id=device, device_id_type=MESH)

    def answered(which):
        there, device, _ = others[which]

        @pl.when(there & later(device))
        def _():
            pl.semaphore_wait(answer.at[which], 1)

    def group_answered(stage):
        @pl.when(place[stage] < sizes[stage] - 1)
        def _():
            pl.semaphore_wait(group_answer.at[stage], sizes[stage] - 1 - place[stage])

    def rows(c, size=CHUNK):
        return pl.ds(pl.multiple_of(c * size, size), size)

    pieces = rows_a // PIECE

    def load(i):
        src = a_ref.at[rows(i, PIECE)] if i < pieces else v_ref
        size = PIECE if i < pieces else rows_v
        return pltpu.make_async_copy(src, held.at[pl.ds(i * PIECE, size)], in_sem.at[i])

    for i in range(pieces + 1):
        load(i).start()

    def add_gram(x):
        high, low = halves(x)
        hh[...] += bdot(high, high, 0, 0)
        hl[...] += bdot(high, low, 0, 0)

    def clear_gram():
        hh[...] = jnp.zeros_like(hh)
        hl[...] = jnp.zeros_like(hl)

    def sum_over_row(rnd, between):
        cross = hl[...]
        gram = hh[...] + (cross + cross.T)
        part[rnd, 0, pl.ds(0, 128), :] = gram[:128, :128]
        part[rnd, 0, pl.ds(128, 64), :] = gram[:64, 128:]
        part[rnd, 1, pl.ds(0, 64), :] = gram[64:128, 128:]
        part[rnd, 1, pl.ds(64, 128), :] = gram[128:, 128:]

        def move(step, src, dst, device):
            return remote(src, dst, sum_s.at[rnd, step], sum_r.at[rnd, step], device)

        copy = move(0, part.at[rnd, 1 - core], near.at[rnd], (p, beside))
        copy.start()
        copy.wait()
        half[rnd] = part[rnd, core] + near[rnd]
        copy = move(1, half.at[rnd], far.at[rnd], (p, across))
        copy.start()
        between()
        copy.wait()
        full[rnd, core] = half[rnd] + far[rnd]
        copy = move(2, full.at[rnd, core], full.at[rnd, core], (p, beside))
        copy.start()
        copy.wait()
        top = full[rnd, 0, pl.ds(0, 128), :]
        mid = jnp.concatenate([full[rnd, 0, pl.ds(128, 64), :], full[rnd, 1, pl.ds(0, 64), :]], axis=0)
        low = full[rnd, 1, pl.ds(64, 128), :]
        return jnp.concatenate(
            [jnp.concatenate([top, mid], axis=1), jnp.concatenate([mid.T, low], axis=1)], axis=0
        )

    def off_mass(gram):
        row = lax.broadcasted_iota(jnp.int32, (WIDE, WIDE), 0)
        col = lax.broadcasted_iota(jnp.int32, (WIDE, WIDE), 1)
        squares = jnp.where(row == col, 0.0, gram * gram)
        return jnp.sum(jnp.sum(squares, axis=1, keepdims=True), axis=0, keepdims=True)

    def take_turn(gram):
        turn = rotation(gram * gram_scale, s, splat)
        high, low = halves(turn)
        qh[...] = high
        ql[...] = low
        return turn

    def turned(x, qh=qh, ql=ql):
        high, low = halves(x)
        return bdot(low, qh[...], 1, 0) + bdot(high, ql[...], 1, 0) + bdot(high, qh[...], 1, 0)

    def chunk(c):
        return c, rows(c)

    def small_chunk(v):
        return chunks_a + v, pl.ds(pl.multiple_of(rows_a + v * SMALL, SMALL), SMALL)

    def up(c):
        src, dst = sent.at[up_from, c[1]], got.at[0, c[1]]
        return remote(src, dst, up_s.at[c[0]], up_r.at[c[0]], (p + 1, r))

    def down(c):
        src, dst = sent.at[1, c[1]], got.at[1, c[1]]
        return remote(src, dst, dn_s.at[c[0]], dn_r.at[c[0]], (p - 1, r))

    def raw_copy(i):
        at = pl.ds(0, RAW_FIRST) if i == 0 else pl.ds(RAW_FIRST, RAW * CHUNK - RAW_FIRST)
        return remote(a_ref.at[at], raw.at[at], raw_s.at[i], raw_r.at[i], (mate, r))

    def relay(c):
        return remote(relayed.at[rows(c)], got.at[odd, rows(c)], rel_s.at[c], rel_r.at[c], (to, r))

    def turn_copy(step):
        if step == 0:
            return remote(q_out.at[core], q_in.at[core], turn_s.at[0], turn_r.at[0], (mate, r))
        return remote(q_in.at[core], q_in.at[core], turn_s.at[1], turn_r.at[1], (p, beside))

    def send_up(c):
        @pl.when(has_up)
        def _():
            up(c).start()

    def send_down(c):
        @pl.when(has_dn)
        def _():
            down(c).start()

    def send_all(lo, hi, make, before=lambda c: None):
        @pl.loop(lo, hi)
        def _(c):
            before(c)
            send_up(make(c))

            @pl.when(jnp.logical_not(last_of_line))
            def _():
                send_down(make(c))

        @pl.when(last_of_line)
        def _():
            @pl.loop(lo, hi)
            def _(c):
                send_down(make(c))

    def receive(c):
        @pl.when(has_dn)
        def _():
            up(c).wait_recv()

        @pl.when(has_up)
        def _():
            down(c).wait_recv()

    def keep_ends(at, y):
        @pl.when(p == 0)
        def _():
            got[0, at, :] = y[:, :BLK]

        @pl.when(p == pairs - 1)
        def _():
            got[1, at, :] = y[:, :BLK]

    def turn_rows(at):
        y = turned(held[at, :])
        sent[0, at, :] = y[:, :BLK]
        sent[1, at, :] = y[:, BLK:]
        keep_ends(at, y)

    def arrived(at):
        return jnp.concatenate([got[0, at, :], got[1, at, :]], axis=1)

    def group_copy(stage, k):
        here = place[stage]
        other = lax.rem(here + k, sizes[stage])
        dst = groups.at[stage, here]
        return remote(mine.at[stage], dst, grp_s.at[stage, k], grp_r.at[stage, here], group_device(stage, other))

    def group_send(stage, value):
        group_answered(stage)
        mine[stage] = value
        groups[stage, place[stage]] = value
        for k in range(1, sizes[stage]):
            group_copy(stage, k).start()

    def group_sum(stage):
        for k in range(1, sizes[stage]):
            other = lax.rem(place[stage] + k, sizes[stage])
            dst = groups.at[stage, other]
            remote(
                mine.at[stage], dst, grp_s.at[stage, k], grp_r.at[stage, other], group_device(stage, other)
            ).wait_recv()
        total = groups[stage, 0]
        for other in range(1, sizes[stage]):
            total = total + groups[stage, other]
        return total

    clear_gram()
    for i in range(pieces):
        load(i).wait()
        if i == pieces // 2:
            barrier()
            raw_copy(0).start()
        add_gram(held[rows(i, PIECE), :])

    def rest_of_raw():
        raw_copy(1).start()

    gram = sum_over_row(0, rest_of_raw)
    mass_one = off_mass(gram)
    turn = take_turn(gram)
    q_out[0] = turn[:BLK]
    q_out[1] = turn[BLK:]
    turn_copy(0).start()

    answered(0)
    send_all(RAW, chunks_a, chunk, lambda c: turn_rows(rows(c)))

    turn_copy(0).wait_recv()
    turn_copy(1).start()
    turn_copy(1).wait()
    for i in range(2):
        high, low = halves(q_in[i])
        ph[pl.ds(i * BLK, BLK), :] = high
        pl_[pl.ds(i * BLK, BLK), :] = low

    raw_copy(0).wait_recv()
    raw_copy(1).wait_recv()
    answered(1)
    answered(2)

    @pl.loop(0, RAW)
    def _(c):
        y = turned(raw[rows(c), :], ph, pl_)
        top, bottom = y[:, :BLK], y[:, BLK:]
        got[1 - odd, rows(c), :] = jnp.where((odd == 0) | (p == 1), bottom, top)
        relayed[rows(c), :] = jnp.where(odd == 0, top, bottom)

        @pl.when(has_to)
        def _():
            relay(c).start()

        @pl.when((p == 0) | (p == pairs - 1))
        def _():
            keep_ends(rows(c), turned(held[rows(c), :]))

    load(pieces).wait()

    @pl.loop(0, rows_v // PIECE)
    def _(c):
        turn_rows(pl.ds(pl.multiple_of(rows_a + c * PIECE, PIECE), PIECE))

    send_all(0, EARLY, small_chunk)

    clear_gram()

    @pl.loop(0, RAW)
    def _(c):
        @pl.when(has_source)
        def _():
            relay(c).wait_recv()

        add_gram(arrived(rows(c)))

    @pl.loop(RAW, chunks_a)
    def _(c):
        receive(chunk(c))
        add_gram(arrived(rows(c)))

    def some_vectors():
        send_all(EARLY, EARLY + MIDDLE, small_chunk)

    gram = sum_over_row(1, some_vectors)
    mass_two = off_mass(gram)
    first = lax.broadcasted_iota(jnp.int32, (8, 128), 1) == 0
    both = jnp.where(first, jnp.broadcast_to(mass_one, (8, 128)), jnp.broadcast_to(mass_two, (8, 128)))
    group_send(0, both)

    send_all(EARLY + MIDDLE, small, small_chunk)

    take_turn(gram)
    group_send(1, group_sum(0))

    pieces_v = rows_v // SMALL

    def out(c):
        return pltpu.make_async_copy(done.at[rows(c, PIECE)], ao_ref.at[rows(c, PIECE)], out_sem.at[c])

    def out_v(v):
        return pltpu.make_async_copy(done.at[small_chunk(v)[1]], vo_ref.at[rows(v, SMALL)], out_sem.at[pieces + v])

    @pl.loop(0, pieces)
    def _(c):
        done[rows(c, PIECE), :] = turned(arrived(rows(c, PIECE)))
        out(c).start()

    @pl.loop(0, pieces_v)
    def _(v):
        receive(small_chunk(v))
        at = small_chunk(v)[1]
        done[at, :] = turned(arrived(at))
        out_v(v).start()

    m_ref[...] = group_sum(1) * mass_scale

    def sent_all(c):
        @pl.when(has_up)
        def _():
            up(c).wait_send()

        @pl.when(has_dn)
        def _():
            down(c).wait_send()

    @pl.loop(RAW, chunks_a)
    def _(c):
        sent_all(chunk(c))

    @pl.loop(0, small)
    def _(v):
        sent_all(small_chunk(v))

    raw_copy(0).wait_send()
    raw_copy(1).wait_send()

    @pl.loop(0, RAW)
    def _(c):
        @pl.when(has_to)
        def _():
            relay(c).wait_send()

    turn_copy(0).wait_send()
    for stage in range(2):
        for k in range(1, sizes[stage]):
            group_copy(stage, k).wait_send()

    @pl.loop(0, pieces)
    def _(c):
        out(c).wait()

    @pl.loop(0, pieces_v)
    def _(v):
        out_v(v).wait()


def local(pairs, matrix, vectors):
    rows_a, rows_v = matrix.shape[0], vectors.shape[0]
    total_rows = float(rows_a * lax.axis_size("row"))
    sends = rows_a // CHUNK + rows_v // SMALL
    body = functools.partial(kernel, pairs, 2.0**-13, 1.0 / (total_rows * total_rows * float(pairs)))
    dma = pltpu.SemaphoreType.DMA
    vmem = pltpu.VMEM
    matrix_out, vectors_out, mass = pl.pallas_call(
        body,
        out_shape=(
            jax.ShapeDtypeStruct(matrix.shape, F32),
            jax.ShapeDtypeStruct(vectors.shape, F32),
            jax.ShapeDtypeStruct((8, 128), F32),
        ),
        in_specs=[pl.BlockSpec(memory_space=pltpu.HBM)] * 2,
        out_specs=(
            pl.BlockSpec(memory_space=pl.ANY),
            pl.BlockSpec(memory_space=pl.ANY),
            pl.BlockSpec(memory_space=vmem),
        ),
        scratch_shapes=[
            vmem((rows_a + rows_v, WIDE), F32),
            vmem((2, rows_a + rows_v, BLK), F32),
            vmem((2, rows_a + rows_v, BLK), F32),
            vmem((rows_a + rows_v, WIDE), F32),
            vmem((RAW * CHUNK, WIDE), F32),
            vmem((RAW * CHUNK, BLK), F32),
            vmem((WIDE, WIDE), F32),
            vmem((8, 8, 128), F32),
            vmem((WIDE, WIDE), F32),
            vmem((WIDE, WIDE), F32),
            vmem((WIDE, WIDE), jnp.bfloat16),
            vmem((WIDE, WIDE), jnp.bfloat16),
            vmem((WIDE, WIDE), jnp.bfloat16),
            vmem((WIDE, WIDE), jnp.bfloat16),
            vmem((2, BLK, WIDE), F32),
            vmem((2, BLK, WIDE), F32),
            vmem((2, 2, 192, 128), F32),
            vmem((2, 192, 128), F32),
            vmem((2, 192, 128), F32),
            vmem((2, 192, 128), F32),
            vmem((2, 2, 192, 128), F32),
            vmem((2, 8, 128), F32),
            vmem((2, 8, 8, 128), F32),
            pltpu.SemaphoreType.REGULAR((3,)),
            pltpu.SemaphoreType.REGULAR((2,)),
            dma((rows_a // PIECE + 1,)),
            dma((sends,)),
            dma((sends,)),
            dma((sends,)),
            dma((sends,)),
            dma((2,)),
            dma((2,)),
            dma((RAW,)),
            dma((RAW,)),
            dma((2,)),
            dma((2,)),
            dma((2, 3)),
            dma((2, 3)),
            dma((2, 8)),
            dma((2, 8)),
            dma((rows_a // PIECE + rows_v // SMALL,)),
        ],
        compiler_params=pltpu.CompilerParams(
            collective_id=0, has_side_effects=True, vmem_limit_bytes=48 * 2**20
        ),
    )(matrix, vectors)
    return matrix_out, vectors_out, mass[0, :2]


def solution(mesh):
    return jax.shard_map(
        functools.partial(local, mesh.shape["pair"]),
        mesh=mesh,
        in_specs=(P("row", "pair"), P("row", "pair")),
        out_specs=(P("row", "pair"), P("row", "pair"), P()),
        check_vma=False,
    )
```

```python
import functools

import jax
import jax.numpy as jnp
from jax import lax
from jax.experimental import pallas as pl
from jax.experimental.pallas import tpu as pltpu
from jax.sharding import PartitionSpec as P

HIGH = lax.Precision.HIGHEST
MESH = pl.DeviceIdType.MESH
F32 = jnp.float32
BLK = 128
WIDE = 2 * BLK
OUTER = 32
PIECE = 512
CHUNK = 256
SMALL = 128
RAW = 3
RAW_FIRST = 128
EARLY = 2
MIDDLE = 1


def dot(a, b, ca, cb):
    dims = (((ca,), (cb,)), ((), ()))
    return lax.dot_general(a, b, dims, precision=HIGH, preferred_element_type=F32)


def bdot(a, b, ca, cb):
    dims = (((ca,), (cb,)), ((), ()))
    return lax.dot_general(a, b, dims, preferred_element_type=F32)


def halves(a):
    high = a.astype(jnp.bfloat16)
    return high, (a - high.astype(F32)).astype(jnp.bfloat16)


def dot3(a, b, ca, cb):
    ah, al = halves(a)
    bh, bl = halves(b)
    return bdot(al, bh, ca, cb) + bdot(ah, bl, ca, cb) + bdot(ah, bh, ca, cb)


def wide(v):
    return jnp.concatenate([v] * (WIDE // 128), axis=1)


def panel(s, splat, k, end):
    c0 = (k // 128) * 128
    own = s[pl.ds(k, 8), pl.ds(c0, 128)]
    for j in range(8):
        at = k - c0 + j
        splat[j] = jnp.broadcast_to(own[:, at : at + 1], (8, 128))
    e = {(i, j): splat[j, i : i + 1, :] for j in range(8) for i in range(j, 8)}
    lanes = lax.broadcasted_iota(jnp.int32, (1, WIDE), 1)
    rows = []
    for i in range(8):
        row = s[pl.ds(k + i, 1), :]
        row = jnp.where((lanes >= k) & (lanes < k + 8), 0.0, row)
        rows.append(jnp.where(lanes == k + i, 1.0, row))
    l = {}
    scale = []
    for a in range(0, 8, 2):
        b = a + 1
        p, q, t = e[a, a], e[b, a], e[b, b]
        ra, rd = lax.rsqrt(p), lax.rsqrt(p * t - q * q)
        rb = rd * (p * ra)
        scale += [ra, rb]
        l[b, a] = q * ra
        for i in range(b + 1, 8):
            l[i, a] = e[i, a] * ra
            l[i, b] = (e[i, b] - l[i, a] * l[b, a]) * rb
        for j in range(b + 1, 8):
            for i in range(j, 8):
                e[i, j] = e[i, j] - (l[i, a] * l[j, a] + l[i, b] * l[j, b])
        rows[a] = rows[a] * wide(ra)
        rows[b] = (rows[b] - wide(l[b, a]) * rows[a]) * wide(rb)
        for i in range(b + 1, 8):
            rows[i] = rows[i] - (wide(l[i, a]) * rows[a] + wide(l[i, b]) * rows[b])
    for i in range(8):
        s[pl.ds(k + i, 1), :] = rows[i]
    full = [jnp.broadcast_to(row, (8, WIDE)) for row in rows]
    lanes = lax.broadcasted_iota(jnp.int32, (8, WIDE), 1)
    inside = (lanes >= k) & (lanes < k + 8)
    for g in range(k + 8, end, 8):
        old = s[pl.ds(g, 8), :]
        m = []
        for j in range(8):
            at = k + j
            t = jnp.broadcast_to(old[:, at : at + 1], (8, 128))
            for jj in range(j):
                t = t - m[jj] * jnp.broadcast_to(l[j, jj], (8, 128))
            m.append(t * jnp.broadcast_to(scale[j], (8, 128)))
        new = jnp.where(inside, 0.0, old)
        for j in range(8):
            new = new - wide(m[j]) * full[j]
        s[pl.ds(g, 8), :] = new


def factor_inverse(s, splat):
    for b0 in range(0, WIDE, OUTER):
        b1 = b0 + OUTER
        for k in range(b0, b1, 8):
            panel(s, splat, k, b1)
        if b1 == WIDE:
            break
        lanes = lax.broadcasted_iota(jnp.int32, (OUTER, WIDE), 1)
        row = lax.broadcasted_iota(jnp.int32, (OUTER, WIDE), 0)
        block = jnp.where((lanes < b1) & (lanes > row + b0), 0.0, s[pl.ds(b0, OUTER), :])
        rest = s[pl.ds(b1, WIDE - b1), :]
        c0 = (b0 // 128) * 128
        near = lax.broadcasted_iota(jnp.int32, (1, 128), 1) + c0
        inverse = jnp.where((near >= b0) & (near < b1), block[:, c0 : c0 + 128], 0.0)
        factor = dot3(rest[:, c0 : c0 + 128], inverse, 1, 1)
        lanes = lax.broadcasted_iota(jnp.int32, (1, WIDE), 1)
        rest = jnp.where((lanes >= b0) & (lanes < b1), 0.0, rest)
        s[pl.ds(b1, WIDE - b1), :] = rest - dot3(factor, block, 1, 0)


def rotation(gram, s, splat):
    square = dot(gram, gram, 1, 0)
    s[...] = dot(square, square, 1, 0)
    factor_inverse(s, splat)
    row = lax.broadcasted_iota(jnp.int32, (WIDE, WIDE), 0)
    col = lax.broadcasted_iota(jnp.int32, (WIDE, WIDE), 1)
    turn = dot(square, jnp.where(row >= col, s[...], 0.0), 1, 1)
    for product in (dot3, dot):
        over = product(turn, turn, 0, 0)
        over = jnp.where(row == col, (over - 1.0) * 0.5, jnp.where(row < col, over, 0.0))
        turn = turn - dot3(turn, over, 1, 0)
    return turn


def kernel(
    pairs, gram_scale, mass_scale,
    a_ref, v_ref, ao_ref, vo_ref, m_ref,
    held, sent, got, done, raw, relayed, s, splat, hh, hl, qh, ql, ph, pl_, q_out, q_in,
    part, near, half, far, full, mine, groups,
    answer, group_answer, in_sem, up_s, up_r, dn_s, dn_r, raw_s, raw_r, rel_s, rel_r, turn_s, turn_r, sum_s, sum_r, grp_s, grp_r, out_sem,
):
    rows_a, rows_v = a_ref.shape[0], v_ref.shape[0]
    chunks_a, small = rows_a // CHUNK, rows_v // SMALL
    inner = min(8, pairs)
    outer = pairs // inner
    p, r = lax.axis_index("pair"), lax.axis_index("row")
    core = lax.rem(r, 2)
    beside = r + 1 - 2 * core
    across = lax.rem(r + 2, 4)
    odd = lax.rem(p, 2)
    mate = p + 1 - 2 * odd
    to = p + 2 - 4 * odd
    source = p - 2 + 4 * odd
    beyond = p - 1 + 2 * odd
    pa, pb = p // inner, lax.rem(p, inner)
    halves_z = 2 - outer % 2
    count_y = outer // halves_z
    pm = lax.rem(pa, halves_z) * count_y + pa // halves_z
    line = inner * halves_z
    up_from = (pairs - p) // pairs
    has_up, has_dn = p < pairs - 1, p > 0
    has_to = (to >= 0) & (to < pairs)
    has_source = (source >= 0) & (source < pairs)
    has_beyond = (beyond >= 0) & (beyond < pairs)
    last_of_line = (lax.rem(p, line) == line - 1) & (p < pairs - 1)

    def group_device(stage, other):
        if stage == 0:
            return (pa * inner + other, r)
        return ((lax.rem(other, count_y) * halves_z + other // count_y) * inner + pb, r)

    sizes, place = (inner, outer), (pb, pm)

    def later(other):
        return (other > p) == (other // line == p // line)

    def remote(src, dst, send_sem, recv_sem, device):
        return pltpu.make_async_remote_copy(
            src_ref=src, dst_ref=dst, send_sem=send_sem, recv_sem=recv_sem, device_id=device, device_id_type=MESH
        )

    bar = pltpu.get_barrier_semaphore()

    def hello(device):
        pl.semaphore_signal(bar, 1, device_id=device, device_id_type=MESH)

    hello((p, beside))
    hello((p, across))
    hello((mate, r))
    others = ((has_beyond, beyond, 0), (has_to, to, 2), (has_source, source, 1))
    for there, device, _ in others:

        @pl.when(there & later(device))
        def _(device=device):
            hello((device, r))

    def group_peers():
        for stage in range(2):
            for k in range(1, sizes[stage]):
                yield stage, lax.rem(place[stage] + k, sizes[stage])

    for stage, other in group_peers():

        @pl.when(other > place[stage])
        def _(stage=stage, other=other):
            hello(group_device(stage, other))

    def barrier():
        count = 3 + pb + pm
        for there, device, _ in others:
            count = count + jnp.where(there & jnp.logical_not(later(device)), 1, 0)
        pl.semaphore_wait(bar, count)
        for there, device, which in others:

            @pl.when(there & jnp.logical_not(later(device)))
            def _(device=device, which=which):
                pl.semaphore_signal(answer.at[which], 1, device_id=(device, r), device_id_type=MESH)

        for stage, other in group_peers():

            @pl.when(other < place[stage])
            def _(stage=stage, other=other):
                device = group_device(stage, other)
                pl.semaphore_signal(group_answer.at[stage], 1, device_id=device, device_id_type=MESH)

    def answered(which):
        there, device, _ = others[which]

        @pl.when(there & later(device))
        def _():
            pl.semaphore_wait(answer.at[which], 1)

    def group_answered(stage):
        @pl.when(place[stage] < sizes[stage] - 1)
        def _():
            pl.semaphore_wait(group_answer.at[stage], sizes[stage] - 1 - place[stage])

    def rows(c, size=CHUNK):
        return pl.ds(pl.multiple_of(c * size, size), size)

    pieces = rows_a // PIECE

    def load(i):
        src = a_ref.at[rows(i, PIECE)] if i < pieces else v_ref
        size = PIECE if i < pieces else rows_v
        return pltpu.make_async_copy(src, held.at[pl.ds(i * PIECE, size)], in_sem.at[i])

    for i in range(pieces + 1):
        load(i).start()

    def add_gram(x):
        high, low = halves(x)
        hh[...] += bdot(high, high, 0, 0)
        hl[...] += bdot(high, low, 0, 0)

    def clear_gram():
        hh[...] = jnp.zeros_like(hh)
        hl[...] = jnp.zeros_like(hl)

    def sum_over_row(rnd, between):
        cross = hl[...]
        gram = hh[...] + (cross + cross.T)
        part[rnd, 0, pl.ds(0, 128), :] = gram[:128, :128]
        part[rnd, 0, pl.ds(128, 64), :] = gram[:64, 128:]
        part[rnd, 1, pl.ds(0, 64), :] = gram[64:128, 128:]
        part[rnd, 1, pl.ds(64, 128), :] = gram[128:, 128:]

        def move(step, src, dst, device):
            return remote(src, dst, sum_s.at[rnd, step], sum_r.at[rnd, step], device)

        copy = move(0, part.at[rnd, 1 - core], near.at[rnd], (p, beside))
        copy.start()
        copy.wait()
        half[rnd] = part[rnd, core] + near[rnd]
        copy = move(1, half.at[rnd], far.at[rnd], (p, across))
        copy.start()
        between()
        copy.wait()
        full[rnd, core] = half[rnd] + far[rnd]
        copy = move(2, full.at[rnd, core], full.at[rnd, core], (p, beside))
        copy.start()
        copy.wait()
        top = full[rnd, 0, pl.ds(0, 128), :]
        mid = jnp.concatenate([full[rnd, 0, pl.ds(128, 64), :], full[rnd, 1, pl.ds(0, 64), :]], axis=0)
        low = full[rnd, 1, pl.ds(64, 128), :]
        return jnp.concatenate(
            [jnp.concatenate([top, mid], axis=1), jnp.concatenate([mid.T, low], axis=1)], axis=0
        )

    def off_mass(gram):
        row = lax.broadcasted_iota(jnp.int32, (WIDE, WIDE), 0)
        col = lax.broadcasted_iota(jnp.int32, (WIDE, WIDE), 1)
        squares = jnp.where(row == col, 0.0, gram * gram)
        return jnp.sum(jnp.sum(squares, axis=1, keepdims=True), axis=0, keepdims=True)

    def take_turn(gram):
        turn = rotation(gram * gram_scale, s, splat)
        high, low = halves(turn)
        qh[...] = high
        ql[...] = low
        return turn

    def turned(x, qh=qh, ql=ql):
        high, low = halves(x)
        return bdot(low, qh[...], 1, 0) + bdot(high, ql[...], 1, 0) + bdot(high, qh[...], 1, 0)

    def chunk(c):
        return c, rows(c)

    def small_chunk(v):
        return chunks_a + v, pl.ds(pl.multiple_of(rows_a + v * SMALL, SMALL), SMALL)

    def up(c):
        src, dst = sent.at[up_from, c[1]], got.at[0, c[1]]
        return remote(src, dst, up_s.at[c[0]], up_r.at[c[0]], (p + 1, r))

    def down(c):
        src, dst = sent.at[1, c[1]], got.at[1, c[1]]
        return remote(src, dst, dn_s.at[c[0]], dn_r.at[c[0]], (p - 1, r))

    def raw_copy(i):
        at = pl.ds(0, RAW_FIRST) if i == 0 else pl.ds(RAW_FIRST, RAW * CHUNK - RAW_FIRST)
        return remote(a_ref.at[at], raw.at[at], raw_s.at[i], raw_r.at[i], (mate, r))

    def relay(c):
        return remote(relayed.at[rows(c)], got.at[odd, rows(c)], rel_s.at[c], rel_r.at[c], (to, r))

    def turn_copy(step):
        if step == 0:
            return remote(q_out.at[core], q_in.at[core], turn_s.at[0], turn_r.at[0], (mate, r))
        return remote(q_in.at[core], q_in.at[core], turn_s.at[1], turn_r.at[1], (p, beside))

    def send_up(c):
        @pl.when(has_up)
        def _():
            up(c).start()

    def send_down(c):
        @pl.when(has_dn)
        def _():
            down(c).start()

    def send_all(lo, hi, make, before=lambda c: None):
        @pl.loop(lo, hi)
        def _(c):
            before(c)
            send_up(make(c))

            @pl.when(jnp.logical_not(last_of_line))
            def _():
                send_down(make(c))

        @pl.when(last_of_line)
        def _():
            @pl.loop(lo, hi)
            def _(c):
                send_down(make(c))

    def receive(c):
        @pl.when(has_dn)
        def _():
            up(c).wait_recv()

        @pl.when(has_up)
        def _():
            down(c).wait_recv()

    def keep_ends(at, y):
        @pl.when(p == 0)
        def _():
            got[0, at, :] = y[:, :BLK]

        @pl.when(p == pairs - 1)
        def _():
            got[1, at, :] = y[:, :BLK]

    def turn_rows(at):
        y = turned(held[at, :])
        sent[0, at, :] = y[:, :BLK]
        sent[1, at, :] = y[:, BLK:]
        keep_ends(at, y)

    def arrived(at):
        return jnp.concatenate([got[0, at, :], got[1, at, :]], axis=1)

    def group_copy(stage, k):
        here = place[stage]
        other = lax.rem(here + k, sizes[stage])
        dst = groups.at[stage, here]
        return remote(mine.at[stage], dst, grp_s.at[stage, k], grp_r.at[stage, here], group_device(stage, other))

    def group_send(stage, value):
        group_answered(stage)
        mine[stage] = value
        groups[stage, place[stage]] = value
        for k in range(1, sizes[stage]):
            group_copy(stage, k).start()

    def group_sum(stage):
        for k in range(1, sizes[stage]):
            other = lax.rem(place[stage] + k, sizes[stage])
            dst = groups.at[stage, other]
            remote(
                mine.at[stage], dst, grp_s.at[stage, k], grp_r.at[stage, other], group_device(stage, other)
            ).wait_recv()
        total = groups[stage, 0]
        for other in range(1, sizes[stage]):
            total = total + groups[stage, other]
        return total

    clear_gram()
    for i in range(pieces):
        load(i).wait()
        if i == pieces // 2:
            barrier()
            raw_copy(0).start()
        add_gram(held[rows(i, PIECE), :])

    def rest_of_raw():
        raw_copy(1).start()

    gram = sum_over_row(0, rest_of_raw)
    mass_one = off_mass(gram)
    turn = take_turn(gram)
    q_out[0] = turn[:BLK]
    q_out[1] = turn[BLK:]
    turn_copy(0).start()

    answered(0)
    send_all(RAW, chunks_a, chunk, lambda c: turn_rows(rows(c)))

    turn_copy(0).wait_recv()
    turn_copy(1).start()
    turn_copy(1).wait()
    for i in range(2):
        high, low = halves(q_in[i])
        ph[pl.ds(i * BLK, BLK), :] = high
        pl_[pl.ds(i * BLK, BLK), :] = low

    raw_copy(0).wait_recv()
    raw_copy(1).wait_recv()
    answered(1)
    answered(2)

    @pl.loop(0, RAW)
    def _(c):
        y = turned(raw[rows(c), :], ph, pl_)
        top, bottom = y[:, :BLK], y[:, BLK:]
        got[1 - odd, rows(c), :] = jnp.where((odd == 0) | (p == 1), bottom, top)
        relayed[rows(c), :] = jnp.where(odd == 0, top, bottom)

        @pl.when(has_to)
        def _():
            relay(c).start()

        @pl.when((p == 0) | (p == pairs - 1))
        def _():
            keep_ends(rows(c), turned(held[rows(c), :]))

    load(pieces).wait()

    @pl.loop(0, rows_v // PIECE)
    def _(c):
        turn_rows(pl.ds(pl.multiple_of(rows_a + c * PIECE, PIECE), PIECE))

    send_all(0, EARLY, small_chunk)

    clear_gram()

    @pl.loop(0, RAW)
    def _(c):
        @pl.when(has_source)
        def _():
            relay(c).wait_recv()

        add_gram(arrived(rows(c)))

    @pl.loop(RAW, chunks_a)
    def _(c):
        receive(chunk(c))
        add_gram(arrived(rows(c)))

    def some_vectors():
        send_all(EARLY, EARLY + MIDDLE, small_chunk)

    gram = sum_over_row(1, some_vectors)
    mass_two = off_mass(gram)
    first = lax.broadcasted_iota(jnp.int32, (8, 128), 1) == 0
    both = jnp.where(first, jnp.broadcast_to(mass_one, (8, 128)), jnp.broadcast_to(mass_two, (8, 128)))
    group_send(0, both)

    send_all(EARLY + MIDDLE, small, small_chunk)

    take_turn(gram)
    group_send(1, group_sum(0))

    pieces_v = rows_v // SMALL

    def out(c):
        return pltpu.make_async_copy(done.at[rows(c, PIECE)], ao_ref.at[rows(c, PIECE)], out_sem.at[c])

    def out_v(v):
        return pltpu.make_async_copy(done.at[small_chunk(v)[1]], vo_ref.at[rows(v, SMALL)], out_sem.at[pieces + v])

    @pl.loop(0, pieces)
    def _(c):
        done[rows(c, PIECE), :] = turned(arrived(rows(c, PIECE)))
        out(c).start()

    @pl.loop(0, pieces_v)
    def _(v):
        receive(small_chunk(v))
        at = small_chunk(v)[1]
        done[at, :] = turned(arrived(at))
        out_v(v).start()

    m_ref[...] = group_sum(1) * mass_scale

    def sent_all(c):
        @pl.when(has_up)
        def _():
            up(c).wait_send()

        @pl.when(has_dn)
        def _():
            down(c).wait_send()

    @pl.loop(RAW, chunks_a)
    def _(c):
        sent_all(chunk(c))

    @pl.loop(0, small)
    def _(v):
        sent_all(small_chunk(v))

    raw_copy(0).wait_send()
    raw_copy(1).wait_send()

    @pl.loop(0, RAW)
    def _(c):
        @pl.when(has_to)
        def _():
            relay(c).wait_send()

    turn_copy(0).wait_send()
    for stage in range(2):
        for k in range(1, sizes[stage]):
            group_copy(stage, k).wait_send()

    @pl.loop(0, pieces)
    def _(c):
        out(c).wait()

    @pl.loop(0, pieces_v)
    def _(v):
        out_v(v).wait()


def local(pairs, matrix, vectors):
    rows_a, rows_v = matrix.shape[0], vectors.shape[0]
    total_rows = float(rows_a * lax.axis_size("row"))
    sends = rows_a // CHUNK + rows_v // SMALL
    body = functools.partial(kernel, pairs, 2.0**-13, 1.0 / (total_rows * total_rows * float(pairs)))
    dma = pltpu.SemaphoreType.DMA
    vmem = pltpu.VMEM
    matrix_out, vectors_out, mass = pl.pallas_call(
        body,
        out_shape=(
            jax.ShapeDtypeStruct(matrix.shape, F32),
            jax.ShapeDtypeStruct(vectors.shape, F32),
            jax.ShapeDtypeStruct((8, 128), F32),
        ),
        in_specs=[pl.BlockSpec(memory_space=pltpu.HBM)] * 2,
        out_specs=(
            pl.BlockSpec(memory_space=pl.ANY),
            pl.BlockSpec(memory_space=pl.ANY),
            pl.BlockSpec(memory_space=vmem),
        ),
        scratch_shapes=[
            vmem((rows_a + rows_v, WIDE), F32),
            vmem((2, rows_a + rows_v, BLK), F32),
            vmem((2, rows_a + rows_v, BLK), F32),
            vmem((rows_a + rows_v, WIDE), F32),
            vmem((RAW * CHUNK, WIDE), F32),
            vmem((RAW * CHUNK, BLK), F32),
            vmem((WIDE, WIDE), F32),
            vmem((8, 8, 128), F32),
            vmem((WIDE, WIDE), F32),
            vmem((WIDE, WIDE), F32),
            vmem((WIDE, WIDE), jnp.bfloat16),
            vmem((WIDE, WIDE), jnp.bfloat16),
            vmem((WIDE, WIDE), jnp.bfloat16),
            vmem((WIDE, WIDE), jnp.bfloat16),
            vmem((2, BLK, WIDE), F32),
            vmem((2, BLK, WIDE), F32),
            vmem((2, 2, 192, 128), F32),
            vmem((2, 192, 128), F32),
            vmem((2, 192, 128), F32),
            vmem((2, 192, 128), F32),
            vmem((2, 2, 192, 128), F32),
            vmem((2, 8, 128), F32),
            vmem((2, 8, 8, 128), F32),
            pltpu.SemaphoreType.REGULAR((3,)),
            pltpu.SemaphoreType.REGULAR((2,)),
            dma((rows_a // PIECE + 1,)),
            dma((sends,)),
            dma((sends,)),
            dma((sends,)),
            dma((sends,)),
            dma((2,)),
            dma((2,)),
            dma((RAW,)),
            dma((RAW,)),
            dma((2,)),
            dma((2,)),
            dma((2, 3)),
            dma((2, 3)),
            dma((2, 8)),
            dma((2, 8)),
            dma((rows_a // PIECE + rows_v // SMALL,)),
        ],
        compiler_params=pltpu.CompilerParams(
            collective_id=0, has_side_effects=True, vmem_limit_bytes=48 * 2**20
        ),
    )(matrix, vectors)
    return matrix_out, vectors_out, mass[0, :2]


def solution(mesh):
    return jax.shard_map(
        functools.partial(local, mesh.shape["pair"]),
        mesh=mesh,
        in_specs=(P("row", "pair"), P("row", "pair")),
        out_specs=(P("row", "pair"), P("row", "pair"), P()),
        check_vma=False,
    )
```
